32 devices in a mesh: dp: 8 (over y, x, core), loop: 4 (over z).
Axes of the slice: x: 2, y: 2, z: 4, core: 2. Of those that a mesh axis runs over, the one named last changes fastest.
Arguments:
- tokens: bfloat16 [3072, 4096], P('dp')
- cotangent: bfloat16 [3072, 4096], P('dp'), may hold values from -6 to 6
- proj_weight: bfloat16 [4096, 4096], P(None, 'dp')
- rotation: float32 [4096, 4096], P('dp', 'loop')
- doc_lengths: int32 [48], P('dp'), may hold values from 1 to 64, as said below
Outputs:
- riemannian: float32 [4096, 4096], P('dp', 'loop')
The draws below stay inside these ranges and needn't reach their ends.
Inputs may be any that keep to these rules, and one draw needn't show every extreme that they name: `doc_lengths`: each slot holds 1 to 64 tokens; some slot holds exactly 64 in every draw.
All inputs are finite; a program needn't handle non-finite values.
Results may differ from the reference program's by a relative error of at most 0.009.
The reference program's roundings to bfloat16 on the way (of `masked`, `rot_half`, `acts_q`, `mixed_q`, `grad_acts` and `grad_mixed`) count: a program that leaves them out, or rounds other values in their place, can miss the bound.
Values may be sent and summed in bfloat16 or wider, within the bound.
No kernel may reach another device: no remote copies, remote signals or barrier semaphores. Data moves between devices by JAX's collectives and lax.ppermute only.
A program may use at most 128 MiB of HBM per device.

```python
import math
import jax
import jax.numpy as jnp
from jax import lax

D = 4096
E = 4096
SLOT = 64
TOKENS = 3072


def draw_tokens(key, part):
    key_values, key_scales = jax.random.split(key, 2)
    row_scales = jnp.exp(jax.random.uniform(key_scales, (TOKENS, 1), jnp.float32, 0.0, math.log(10.0)))
    values = jnp.clip(jax.random.normal(key_values, (TOKENS, D), jnp.float32), -6.0, 6.0)
    return (values * row_scales).astype(jnp.bfloat16)


def draw_proj_weight(key, part):
    key_values, key_scales = jax.random.split(key)
    col_scales = jnp.exp(jax.random.uniform(key_scales, (1, E), jnp.float32, -0.5 * math.log(10.0), 0.5 * math.log(10.0)))
    values = jnp.clip(jax.random.normal(key_values, (D, E), jnp.float32), -6.0, 6.0)
    return (values * col_scales / math.sqrt(D)).astype(jnp.bfloat16)


def draw_rotation(key, part):
    key_rows, key_cols, key_noise = jax.random.split(key, 3)
    row_index = jnp.arange(D, dtype=jnp.int32)[:, None]
    col_index = jnp.arange(D, dtype=jnp.int32)[None, :]
    parity_sum = jnp.zeros((D, D), jnp.int32)
    for bit_place in range(max(D - 1, 1).bit_length()):
        row_bits = jnp.bitwise_and(jnp.right_shift(row_index, bit_place), 1)
        col_bits = jnp.bitwise_and(jnp.right_shift(col_index, bit_place), 1)
        parity_sum = parity_sum + row_bits * col_bits
    parity = parity_sum % 2
    hadamard = 1.0 - 2.0 * parity.astype(jnp.float32)
    row_signs = 1.0 - 2.0 * jax.random.bernoulli(key_rows, 0.5, (D, 1)).astype(jnp.float32)
    col_signs = 1.0 - 2.0 * jax.random.bernoulli(key_cols, 0.5, (1, D)).astype(jnp.float32)
    noise = 0.1 * jnp.clip(jax.random.normal(key_noise, (D, D), jnp.float32), -6.0, 6.0)
    return (row_signs * hadamard * col_signs + noise) / math.sqrt(D)


def draw_doc_lengths(key, part):
    key_lengths, key_pick = jax.random.split(key)
    slot_count = TOKENS // SLOT
    lengths = jax.random.randint(key_lengths, (slot_count,), 1, SLOT + 1, jnp.int32)
    chosen = jax.random.randint(key_pick, (), 0, slot_count, jnp.int32)
    return jnp.where(jnp.arange(slot_count, dtype=jnp.int32) == chosen, SLOT, lengths).astype(jnp.int32)


def block_scale(stream_key, dims, cuts, least, top_value):
    loudness = 1.0
    for axis_at, parts in cuts:
        heights = jax.random.uniform(jax.random.fold_in(jax.random.fold_in(stream_key, 6), axis_at), (parts,), jnp.float32, least / len(cuts), top_value / len(cuts))
        loudness = loudness * jnp.repeat(jnp.exp(heights), dims[axis_at] // parts).reshape((-1,) + (1,) * (len(dims) - 1 - axis_at))
    return loudness


def bell_draw(stream_key, dims, spread, limit, cuts=(), kind=jnp.bfloat16):
    level = block_scale(stream_key, dims, cuts, -0.22, 0.18) if cuts else 1.0
    entries = jax.random.normal(stream_key, dims, jnp.float32) * spread * level
    return jnp.minimum(jnp.maximum(entries, -limit), limit).astype(kind)


def setup_inputs(seed: int = 0) -> dict:
    key_list = jax.random.split(jax.random.key(seed), 6)
    return {
        "tokens": draw_tokens(jax.random.fold_in(key_list[5], 71), 0),
        "cotangent": bell_draw(key_list[1], (TOKENS, E), 1.0, 6.0, ((0, 8),)),
        "proj_weight": draw_proj_weight(jax.random.fold_in(key_list[5], 71), 0),
        "rotation": draw_rotation(jax.random.fold_in(key_list[5], 71), 0),
        "doc_lengths": draw_doc_lengths(jax.random.fold_in(key_list[5], 71), 0),
    }


clip_ratio = 2.0
eps_power = 1e-06

def reference(tokens, cotangent, proj_weight, rotation, doc_lengths):
    positions = jnp.arange(TOKENS, dtype=jnp.int32)
    slot_index = positions // SLOT
    live = positions % SLOT < doc_lengths[slot_index]
    masked = cotangent * live.astype(jnp.bfloat16)[:, None]
    rot_half = rotation.astype(jnp.bfloat16)
    acts = jnp.dot(tokens, rot_half, preferred_element_type=jnp.float32)
    row_limit = clip_ratio * jnp.sqrt(lax.optimization_barrier(jnp.mean(acts * acts, axis=1, keepdims=True)) + eps_power)
    acts_q = jnp.clip(acts, -row_limit, row_limit).astype(jnp.bfloat16)
    mixed = jnp.dot(rot_half.T, proj_weight, preferred_element_type=jnp.float32)
    col_limit = clip_ratio * jnp.sqrt(lax.optimization_barrier(jnp.mean(mixed * mixed, axis=0, keepdims=True)) + eps_power)
    mixed_q = jnp.clip(mixed, -col_limit, col_limit).astype(jnp.bfloat16)
    grad_acts = jnp.dot(masked, mixed_q.T, preferred_element_type=jnp.float32).astype(jnp.bfloat16)
    grad_mixed = jnp.dot(acts_q.T, masked, preferred_element_type=jnp.float32).astype(jnp.bfloat16)
    gradient = jnp.dot(tokens.T, grad_acts, preferred_element_type=jnp.float32)
    gradient = gradient + jnp.dot(proj_weight, grad_mixed.T, preferred_element_type=jnp.float32)
    gradient = gradient * (1.0 / jnp.sqrt(jnp.float32(TOKENS)))
    cross = jnp.dot(gradient.T, rotation, precision=lax.Precision.HIGHEST, preferred_element_type=jnp.float32)
    return gradient - jnp.dot(rotation, cross, precision=lax.Precision.HIGHEST, preferred_element_type=jnp.float32)
```

```python
import jax
import jax.numpy as jnp
from jax import lax
from jax.sharding import PartitionSpec as P

clip_ratio = 2.0
eps_power = 1e-06
cot_limit = 6.0
code_top = 30000.0
BF16 = jnp.bfloat16
F16 = jnp.float16
F32 = jnp.float32


def swap(x, mask):
    n = lax.axis_size("dp")
    return lax.ppermute(x, "dp", [(i, i ^ mask) for i in range(n)])


def relative_masks():
    half = lax.axis_size("dp") // 2
    return [(q % half) * 2 + q // half for q in range(2 * half)]


def gather_chips(x):
    chips = lax.axis_size("dp") // 2
    if chips == 4:
        half = x.shape[0] // 2
        from_x, from_y = swap(x, 2), swap(x, 4)
        far = [swap(from_x[:half], 4), swap(from_y[half:], 2)]
        return jnp.concatenate([x, from_x, from_y] + far, axis=0)
    bit = 1
    while bit < chips:
        x = jnp.concatenate([x, swap(x, 2 * bit)], axis=0)
        bit *= 2
    return x


def gather(x):
    near = gather_chips(x)
    return jnp.concatenate([near, swap(near, 1)], axis=0)


def gather_small(x):
    return jnp.stack([x] + [swap(x, m) for m in relative_masks()[1:]])


def flip(x, mask):
    n = lax.axis_size("dp")
    place = (mask & 1) * (n // 2) + (mask >> 1)
    width = x.shape[1] // n
    parts = [x[:, (q ^ place) * width : ((q ^ place) + 1) * width] for q in range(n)]
    return jnp.concatenate(parts, axis=1)


def scatter(near, away):
    chips = lax.axis_size("dp") // 2

    def trade(x, mask):
        return flip(swap(x.astype(F16), mask), mask).astype(F32)

    total = near + trade(away, 1)
    size = near.shape[0] // chips
    if chips == 4:
        own, to_x, to_y, far = (total[i * size : (i + 1) * size] for i in range(4))
        half = size // 2
        via_x, via_y = trade(far[:half], 2), trade(far[half:], 4)
        to_y = jnp.concatenate([to_y[:half] + via_x, to_y[half:]], axis=0)
        to_x = jnp.concatenate([to_x[:half], to_x[half:] + via_y], axis=0)
        return own + trade(to_x, 2) + trade(to_y, 4)
    bit = chips // 2
    while bit:
        half = total.shape[0] // 2
        total = total[:half] + trade(total[half:], 2 * bit)
        bit //= 2
    return total


def gather_loop(x):
    n = lax.axis_size("loop")
    up, down = [x], [x]
    for step in range(1, n):
        up.append(lax.ppermute(up[-1], "loop", [(i, i - 1) for i in range(1, n - step + 1)]))
        down.append(lax.ppermute(down[-1], "loop", [(i, i + 1) for i in range(step - 1, n - 1)]))
    me = lax.axis_index("loop")
    return [x] + [jnp.where(me + r < n, up[r], down[n - r]) for r in range(1, n)]


def sum_loop(x):
    n = lax.axis_size("loop")
    bit = 1
    while bit < n:
        x = x + lax.ppermute(x, "loop", [(i, i ^ bit) for i in range(n)])
        bit *= 2
    return x


def dot(a, b, ca, cb):
    return lax.dot_general(a, b, (((ca,), (cb,)), ((), ())), preferred_element_type=F32)


def split(x):
    high = lax.reduce_precision(x, 8, 7)
    return high.astype(BF16), (x - high).astype(BF16)


def half_code(x, scale):
    return lax.reduce_precision(x * scale, 5, 10)


def on_device(tokens, cotangent, proj_weight, rotation, doc_lengths):
    tok_rows, feat_width = tokens.shape
    slot_count = doc_lengths.shape[0]
    slot_len = tok_rows // slot_count
    n, loops = lax.axis_size("dp"), lax.axis_size("loop")
    me, level = lax.axis_index("dp"), lax.axis_index("loop")
    place = (me & 1) * (n // 2) + (me >> 1)
    masks = relative_masks()
    row_block, panel = rotation.shape
    out_block = proj_weight.shape[1]
    all_tokens, all_outs = tok_rows * n, out_block * n
    chunks = max(1, panel // (n * 32))
    wide = panel // chunks
    sub = wide // n

    def relative(x, width, axis):
        cut = [lax.dynamic_slice_in_dim(x, (me ^ m) * width, width, axis) for m in masks]
        return jnp.concatenate(cut, axis=axis)

    rot_top = jnp.maximum(jnp.max(jnp.abs(rotation)), 1e-30)
    rot_unit = rot_top / code_top
    rot_scale = code_top / rot_top
    rot_round = lax.reduce_precision(rotation, 8, 7)
    code = half_code(rotation, rot_scale)
    inner = half_code(rot_round + 0.75 * (rotation - rot_round), rot_scale)
    kept = lax.reduce_precision(code * rot_unit, 8, 7) == rot_round
    rot_code = jnp.where(kept, code, inner).astype(F16)
    rot_units = gather_small(jnp.full((128,), rot_unit))[:, :1]
    rot_parts = [gather(rot_code[:, c * wide : (c + 1) * wide]) for c in range(chunks)]

    def decode(parts):
        return (parts.reshape(n, row_block, -1).astype(F32) * rot_units[:, :, None]).reshape(
            parts.shape
        )

    positions = jnp.arange(tok_rows, dtype=jnp.int32)
    slot_match = (positions // slot_len)[:, None] == jnp.arange(slot_count, dtype=jnp.int32)[
        None, :
    ]
    row_lengths = jnp.sum(jnp.where(slot_match, doc_lengths[None, :], 0), axis=1)
    live_rows = positions % slot_len < row_lengths
    masked = relative(cotangent * live_rows.astype(BF16)[:, None], out_block, 1)
    both = jnp.concatenate(
        [relative(tokens, row_block, 1), relative(proj_weight, row_block, 0).T], axis=0
    )

    share = tok_rows // loops
    own_share = lax.dynamic_slice_in_dim(masked, level * share, share, 0)
    cuts = [own_share[:, q * out_block : (q + 1) * out_block] for q in range(n)]
    cuts = jnp.stack([cuts[0]] + [swap(x, m) for x, m in zip(cuts[1:], masks[1:])])
    shares = jnp.stack(gather_loop(cuts))
    cot_owned = jnp.concatenate(
        [
            lax.dynamic_index_in_dim(shares, (a - level) % loops, 0, keepdims=False)
            for a in range(loops)
        ],
        axis=1,
    ).reshape(all_tokens, out_block)

    rotated = [dot(both, decode(p).astype(BF16), 1, 0) for p in rot_parts]
    power = sum_loop(sum(jnp.sum(r * r, axis=1) for r in rotated))
    limit = clip_ratio * jnp.sqrt(power / feat_width + eps_power)
    tok_top = jnp.max(jnp.abs(tokens), axis=1).astype(F32)
    weight_top = jnp.max(jnp.abs(proj_weight), axis=0).astype(F32)
    sizes = [
        jnp.sum(limit[tok_rows:] ** 2),
        jnp.sum(limit[:tok_rows] ** 2),
        jnp.sum(tok_top**2),
        jnp.sum(weight_top**2),
        jnp.max(jnp.sum(rotation**2, axis=0)),
    ]
    sizes = jnp.concatenate([jnp.stack(sizes), jnp.zeros((128 - len(sizes),), F32)])
    told = gather_small(jnp.concatenate([limit, sizes]))
    limits = told[:, : limit.shape[0]].astype(BF16)
    norms = jnp.sqrt(n * jnp.max(told[:, limit.shape[0] :], axis=0))
    bound = cot_limit * all_outs**0.5 * (norms[0] * norms[2] + norms[1] * norms[3])
    grad_scale = code_top / jnp.clip(1.02 * bound, 1e-30, 3e38)
    cross_scale = 0.9 / (feat_width**0.5 * jnp.maximum(norms[4], 1e-15))

    acts_limit = limits[:, :tok_rows].reshape(all_tokens, 1)
    mixed_limit = limits[:, tok_rows:].reshape(all_outs, 1)
    acts = [gather(r[:tok_rows].astype(BF16)) for r in rotated]
    mixed = [gather(r[tok_rows:].astype(BF16)) for r in rotated]
    acts_q = [jnp.clip(r, -acts_limit, acts_limit) for r in acts]
    mixed_q = [jnp.clip(r, -mixed_limit, mixed_limit) for r in mixed]
    grad_acts = [dot(masked, m, 1, 0).astype(BF16) for m in mixed_q]
    grad_mixed = [dot(cot_owned, a, 0, 0).astype(BF16) for a in acts_q]

    cols = jnp.arange(wide, dtype=jnp.int32)
    source = ((cols // sub) ^ place) * sub + cols % sub
    shuffle = (cols[:, None] == source[None, :]).astype(BF16)
    to_code = grad_scale / jnp.sqrt(F32(all_tokens))

    rot_high, rot_low = split(decode(jnp.concatenate(rot_parts, axis=1)))
    rows_units = jnp.stack(gather_loop(jnp.full((128,), rot_unit)))[:, :1, None]
    rows_code = jnp.stack(gather_loop(rot_code.T)).astype(F32) * rows_units
    rows_code = rows_code.reshape(loops, chunks, n, sub, row_block)
    rows_code = jnp.concatenate(
        [lax.dynamic_slice_in_dim(rows_code, place ^ q, 1, 2) for q in range(n)], axis=2
    )
    rows_code = rows_code.transpose(1, 2, 0, 3, 4).reshape(chunks, n * loops * sub, row_block)

    strips, correction = [], 0.0
    for c in range(chunks):
        pair = jnp.concatenate([grad_acts[c], grad_mixed[c]], axis=0)
        pair = jnp.dot(pair, shuffle, preferred_element_type=F32).astype(BF16)
        near = dot(pair[:, : wide // 2], both, 0, 0) * to_code
        away = dot(pair[:, wide // 2 :], both, 0, 0) * to_code
        strip = scatter(near, away).astype(F16)
        strips.append(strip)
        rows = jnp.concatenate(gather_loop(strip), axis=0)
        high, low = split(rows.astype(F32))
        stacked = dot(jnp.concatenate([high, low], axis=0), rot_high, 1, 0)
        cross = stacked[: rows.shape[0]] + stacked[rows.shape[0] :] + dot(high, rot_low, 1, 0)
        cross = gather((cross * cross_scale).astype(F16)).astype(F32)
        cross_high, cross_low = split(cross)
        rows_high, rows_low = split(rows_code[c])
        correction = correction + dot(
            jnp.concatenate([rows_high, rows_low, rows_high], axis=0),
            jnp.concatenate([cross_high, cross_high, cross_low], axis=0),
            0,
            0,
        )

    strip = jnp.concatenate(strips, axis=0)
    blocks = [strip[:, q * row_block : (q + 1) * row_block] for q in range(n)]
    blocks = jnp.stack([blocks[0]] + [swap(b, m) for b, m in zip(blocks[1:], masks[1:])])
    blocks = jnp.concatenate(
        [lax.dynamic_slice_in_dim(blocks, place ^ q, 1, 0) for q in range(n)], axis=0
    )
    gradient = blocks.reshape(n, chunks, sub, row_block).transpose(1, 0, 2, 3)
    gradient = gradient.reshape(panel, row_block).T.astype(F32)
    unit = 1.0 / grad_scale
    return gradient * unit - correction * (unit / cross_scale)


def solution(mesh):
    in_specs = (P("dp", None), P("dp", None), P(None, "dp"), P("dp", "loop"), P("dp"))
    out_specs = P("dp", "loop")
    return jax.shard_map(
        on_device, mesh=mesh, in_specs=in_specs, out_specs=out_specs, check_vma=False
    )
```

```python
import jax
import jax.numpy as jnp
from jax import lax
from jax.experimental import pallas as pl
from jax.experimental.pallas import tpu as pltpu
from jax.sharding import PartitionSpec as P

clip_ratio = 2.0
eps_power = 1e-06
cot_limit = 6.0
code_top = 30000.0
BF16 = jnp.bfloat16
F16 = jnp.float16
F32 = jnp.float32


def swap(x, mask):
    n = lax.axis_size("dp")
    return lax.ppermute(x, "dp", [(i, i ^ mask) for i in range(n)])


def relative_masks():
    half = lax.axis_size("dp") // 2
    return [(q % half) * 2 + q // half for q in range(2 * half)]


def gather_small(x):
    bit = 1
    while bit < lax.axis_size("dp") // 2:
        x = jnp.concatenate([x, swap(x, 2 * bit)], axis=0)
        bit *= 2
    return jnp.concatenate([x, swap(x, 1)], axis=0)


def after(x, *earlier):
    return lax.optimization_barrier((x,) + earlier)[0]


def first_step(x):
    return (swap(x, 2), swap(x, 4)) if lax.axis_size("dp") == 8 else ()


def second_step(x, came):
    if lax.axis_size("dp") != 8:
        bit = 1
        while bit < lax.axis_size("dp") // 2:
            x = jnp.concatenate([x, swap(x, 2 * bit)], axis=0)
            bit *= 2
        return x
    half = x.shape[0] // 2
    from_x, from_y = came
    far = [swap(from_x[:half], 4), swap(from_y[half:], 2)]
    return jnp.concatenate([x, from_x, from_y] + far, axis=0)


def trade(x, mask):
    return swap(x.astype(F16), mask).astype(F32)


def scatter_first(total):
    size = total.shape[0] // (lax.axis_size("dp") // 2)
    far = total[3 * size :]
    half = size // 2
    return trade(far[:half], 2), trade(far[half:], 4)


def scatter_last(total, came):
    chips = lax.axis_size("dp") // 2
    if chips != 4:
        bit = chips // 2
        while bit:
            half = total.shape[0] // 2
            total = total[:half] + trade(total[half:], 2 * bit)
            bit //= 2
        return total
    via_x, via_y = came
    size = total.shape[0] // chips
    half = size // 2
    own, to_x, to_y = (total[i * size : (i + 1) * size] for i in range(3))
    to_y = jnp.concatenate([to_y[:half] + via_x, to_y[half:]], axis=0)
    to_x = jnp.concatenate([to_x[:half], to_x[half:] + via_y], axis=0)
    return own + trade(to_x, 2) + trade(to_y, 4)


def exchange_steps(x):
    shape = x.shape
    n = shape[0]
    bits = n.bit_length() - 1

    def halve(x, axis):
        stay, go = jnp.split(x, 2, axis=axis)
        return jnp.concatenate([stay, swap(go, 1 if axis == 0 else n >> axis)], axis=axis)

    x = yield halve(x.reshape((2,) * bits + shape[1:]), 0)
    if bits != 3:
        x = yield halve(x, 1)
        for axis in range(2, bits):
            x = halve(x, axis)
        yield x.reshape(shape)
        return
    upper, lower = jnp.split(x, 2, axis=3)
    upper, lower = yield (halve(upper, 1), halve(lower, 2))
    yield jnp.concatenate([halve(upper, 2), halve(lower, 1)], axis=3).reshape(shape)


def gather_loop(x):
    n = lax.axis_size("loop")

    def turn(r):
        return lax.ppermute(x, "loop", [(i, (i - r) % n) for i in range(n)])

    if n != 4:
        return [x] + [turn(r) for r in range(1, n)]
    me = lax.axis_index("loop")
    after_me, before_me = turn(1), turn(3)
    across = jnp.where(me == 1, after_me, jnp.where(me == 2, before_me, x))
    across = lax.ppermute(across, "loop", [(3, 1), (0, 2), (1, 0), (2, 3)])
    return [x, after_me, across, before_me]


def sum_loop(x):
    n = lax.axis_size("loop")
    bit = 1
    while bit < n:
        x = x + lax.ppermute(x, "loop", [(i, i ^ bit) for i in range(n)])
        bit *= 2
    return x


def dot(a, b, ca, cb):
    return lax.dot_general(a, b, (((ca,), (cb,)), ((), ())), preferred_element_type=F32)


def split(x):
    high = lax.reduce_precision(x, 8, 7)
    return high.astype(BF16), (x - high).astype(BF16)


def half_code(x, scale):
    return lax.reduce_precision(x * scale, 5, 10)


def ordered_call(body, order, grid, ins, in_specs, outs, out_specs):
    return pl.pallas_call(
        body,
        out_shape=outs,
        grid_spec=pltpu.PrefetchScalarGridSpec(
            num_scalar_prefetch=1, grid=grid, in_specs=in_specs, out_specs=out_specs
        ),
        compiler_params=pltpu.CompilerParams(vmem_limit_bytes=32 * 1024 * 1024),
    )(order, *ins)


def lay_both(order, tokens, proj_weight, row_block):
    tok_rows, feat_width = tokens.shape
    outs = proj_weight.shape[1]

    def body(order_ref, tok_ref, weight_ref, placed_ref, plain_ref):
        turned = weight_ref[...].T
        for ref in (placed_ref, plain_ref):
            ref[:tok_rows] = tok_ref[...]
            ref[tok_rows:] = turned

    shape = (tok_rows + outs, feat_width)
    block = (tok_rows + outs, row_block)
    return ordered_call(
        body,
        order,
        (feat_width // row_block,),
        (tokens, proj_weight),
        [
            pl.BlockSpec((tok_rows, row_block), lambda q, o: (0, o[q])),
            pl.BlockSpec((row_block, outs), lambda q, o: (o[q], 0)),
        ],
        [jax.ShapeDtypeStruct(shape, BF16)] * 2,
        [pl.BlockSpec(block, lambda q, o: (0, q)), pl.BlockSpec(block, lambda q, o: (0, o[q]))],
    )


def lay_columns(order, x, live, width):
    def body(order_ref, x_ref, live_ref, out_ref):
        out_ref[...] = (x_ref[...].astype(F32) * live_ref[...]).astype(out_ref.dtype)

    rows, cols = x.shape
    return ordered_call(
        body,
        order,
        (cols // width,),
        (x, live),
        [
            pl.BlockSpec((rows, width), lambda q, o: (0, o[q])),
            pl.BlockSpec((rows, 1), lambda q, o: (0, 0)),
        ],
        jax.ShapeDtypeStruct(x.shape, x.dtype),
        pl.BlockSpec((rows, width), lambda q, o: (0, q)),
    )


def plain_call(body, grid, ins, in_specs, out, out_spec, flops, scratch=()):
    size = sum(x.size * x.dtype.itemsize for x in ins) + out.size * out.dtype.itemsize
    return pl.pallas_call(
        body,
        out_shape=out,
        grid=grid,
        in_specs=in_specs,
        out_specs=out_spec,
        scratch_shapes=scratch,
        compiler_params=pltpu.CompilerParams(vmem_limit_bytes=30 * 1024 * 1024),
        cost_estimate=pl.CostEstimate(flops=flops, bytes_accessed=size, transcendentals=0),
    )(*ins)


def cross_rows(scale, stacked, terms):
    (near_high, near_low), (away_high, away_low) = terms
    rows, depth = stacked.shape[0] // 2, stacked.shape[1]
    cols = near_high.shape[1]
    wide = min(cols, 256)
    half = depth // 2

    def body(scale_ref, rows_ref, nh_ref, nl_ref, ah_ref, al_ref, out_ref):
        wide_part = dot(rows_ref[:, :half], nh_ref[...], 1, 0)
        wide_part += dot(rows_ref[:, half:], ah_ref[...], 1, 0)
        total = wide_part[:rows] + wide_part[rows:]
        total += dot(rows_ref[:rows, :half], nl_ref[...], 1, 0)
        total += dot(rows_ref[:rows, half:], al_ref[...], 1, 0)
        out_ref[...] = total * scale_ref[0, 0]

    panel = pl.BlockSpec((half, wide), lambda j: (0, j))
    return plain_call(
        body,
        (cols // wide,),
        (scale, stacked, near_high, near_low, away_high, away_low),
        [
            pl.BlockSpec(memory_space=pltpu.SMEM),
            pl.BlockSpec((2 * rows, depth), lambda j: (0, 0)),
        ]
        + [panel] * 4,
        jax.ShapeDtypeStruct((rows, cols), F32),
        pl.BlockSpec((rows, wide), lambda j: (0, j)),
        6 * rows * depth * cols,
    )


def add_product(base, factor, levels, chunk, rows, terms):
    (near_high, near_low), (away_high, away_low) = terms
    depth, cols = near_high.shape
    height = base.shape[0]
    loops = rows[0].shape[0]
    wide = min(cols, 256)
    places = lax.axis_size("dp") // 2
    part = depth // loops

    def body(factor_ref, level_ref, base_ref, rh_ref, rl_ref, nh_ref, nl_ref, ah_ref, al_ref, out_ref, kept):
        @pl.when(pl.program_id(0) == 0)
        def _():
            for term, ref in enumerate((rh_ref, rl_ref)):
                for r in range(loops):
                    for h in range(2):
                        kept[term, h, :, r * part : (r + 1) * part] = ref[
                            level_ref[r], :, h * part : (h + 1) * part
                        ]

        def by_level(ref):
            x = ref[...].reshape(places, loops, part // places, wide)
            return jnp.concatenate([x[q, r] for r in range(loops) for q in range(places)], axis=0)

        total = 0.0
        for h, (high_ref, low_ref) in enumerate(((nh_ref, nl_ref), (ah_ref, al_ref))):
            high, low = by_level(high_ref), by_level(low_ref)
            total += dot(kept[0, h], high, 1, 0)
            total += dot(kept[1, h], high, 1, 0)
            total += dot(kept[0, h], low, 1, 0)
        out_ref[...] = base_ref[...] + total * factor_ref[0, 0]

    flat = pl.BlockSpec((height, wide), lambda j: (0, j))
    panel = pl.BlockSpec((depth, wide), lambda j: (0, j))
    strip = pl.BlockSpec((loops, height, 2 * part), lambda j: (0, 0, chunk))
    scalars = pl.BlockSpec(memory_space=pltpu.SMEM)
    return plain_call(
        body,
        (cols // wide,),
        (factor, levels, base, *rows, near_high, near_low, away_high, away_low),
        [scalars, scalars, flat, strip, strip] + [panel] * 4,
        jax.ShapeDtypeStruct(base.shape, F32),
        flat,
        12 * height * depth * cols,
        [pltpu.VMEM((2, 2, height, depth), BF16)],
    )


def on_device(tokens, cotangent, proj_weight, rotation, doc_lengths):
    tok_rows, feat_width = tokens.shape
    slot_count = doc_lengths.shape[0]
    slot_len = tok_rows // slot_count
    n, loops = lax.axis_size("dp"), lax.axis_size("loop")
    half = n // 2
    me, level = lax.axis_index("dp"), lax.axis_index("loop")
    place = (me & 1) * half + (me >> 1)
    masks = relative_masks()
    order = jnp.bitwise_xor(me, jnp.array(masks, jnp.int32))
    places = jnp.bitwise_xor(place, jnp.arange(n, dtype=jnp.int32))
    row_block, panel = rotation.shape
    out_block = proj_weight.shape[1]
    all_tokens, all_outs = tok_rows * n, out_block * n
    chunks = max(1, panel // (n * 64))
    wide = panel // chunks
    sub = wide // n

    rot_top = jnp.maximum(jnp.max(jnp.abs(rotation)), 1e-30)
    rot_power = jnp.floor(14.5 - jnp.log2(rot_top))
    rot_scale, rot_unit = jnp.exp2(rot_power), jnp.exp2(-rot_power)
    rot_round = lax.reduce_precision(rotation, 8, 7)
    code = half_code(rotation, rot_scale)
    inner = half_code(rot_round + 0.75 * (rotation - rot_round), rot_scale)
    read = code * rot_unit
    kept = (lax.reduce_precision(read * (1 + 1e-6), 8, 7) == rot_round) & (
        lax.reduce_precision(read * (1 - 1e-6), 8, 7) == rot_round
    )
    rot_code = jnp.where(kept, code, inner).astype(F16)
    rot_units = jnp.full((128,), rot_unit)
    bit = 1
    while bit < half:
        rot_units = jnp.concatenate([rot_units, swap(rot_units, 2 * bit)], axis=0)
        bit *= 2
    rot_code = after(rot_code, rot_units)
    rot_units = jnp.concatenate([rot_units, swap(rot_units, 1)], axis=0)
    rot_units = rot_units.reshape(2, half, 1, 128)[:, :, :, :1]
    tokens, cotangent, proj_weight = after((tokens, cotangent, proj_weight), rot_code)
    rot_came = first_step(rot_code)

    def decode(part, units):
        part = part.reshape(half, row_block, panel).astype(F32) * units
        return split(part.reshape(half * row_block, panel))

    positions = jnp.arange(tok_rows, dtype=jnp.int32)
    slot_match = (positions // slot_len)[:, None] == jnp.arange(slot_count, dtype=jnp.int32)[
        None, :
    ]
    row_lengths = jnp.sum(jnp.where(slot_match, doc_lengths[None, :], 0), axis=1)
    live_rows = positions % slot_len < row_lengths
    masked = lay_columns(order, cotangent, live_rows.astype(F32)[:, None], out_block)
    both, both_plain = lay_both(order, tokens, proj_weight, row_block)
    cuts = masked.reshape(tok_rows, n, out_block).transpose(1, 0, 2)
    cols = jnp.arange(panel, dtype=jnp.int32)
    source = cols - cols % wide + (((cols % wide) // sub) ^ place) * sub + cols % sub
    shuffle = (cols[:, None] == source[None, :]).astype(BF16)
    rows_terms = [
        dot(x, shuffle, 1, 0).astype(BF16) for x in split(after(rotation, tokens))
    ]
    cuts_way = exchange_steps(cuts)
    cuts = next(cuts_way)
    rot_came = after(rot_came, both, cuts, *rows_terms)
    rows_terms = [lax.all_gather(x, "loop", axis=0) for x in rows_terms]
    rot_near = second_step(rot_code, rot_came)
    rot_away = swap(rot_near, 1)
    rot_terms = [decode(rot_near, rot_units[0])]
    near_part = dot(both[:, : feat_width // 2], rot_terms[0][0], 1, 0)
    cuts = cuts_way.send(after(cuts, *rot_came))

    half_feat, half_out = feat_width // 2, all_outs // 2
    rot_terms.append(decode(after(rot_away, near_part, cuts), rot_units[1]))
    cuts = cuts_way.send(cuts)
    cot_owned = cuts.reshape(2, half * tok_rows, out_block)
    rotated = near_part + dot(both[:, half_feat:], rot_terms[1][0], 1, 0)
    acts_raw, mixed_raw = rotated[:tok_rows].astype(BF16), rotated[tok_rows:].astype(BF16)
    acts_came, mixed_came = first_step(acts_raw), first_step(mixed_raw)
    power = after(jnp.sum(rotated * rotated, axis=1), acts_raw, mixed_raw)
    power = sum_loop(power)
    tokens, proj_weight, rotation = after((tokens, proj_weight, rotation), acts_raw, mixed_raw)
    limit = clip_ratio * jnp.sqrt(power / feat_width + eps_power)
    tok_top = jnp.max(jnp.abs(tokens), axis=1).astype(F32)
    weight_top = jnp.max(jnp.abs(proj_weight), axis=0).astype(F32)
    sizes = [
        jnp.sum(limit[tok_rows:] ** 2),
        jnp.sum(limit[:tok_rows] ** 2),
        jnp.sum(tok_top**2),
        jnp.sum(weight_top**2),
        jnp.max(jnp.sum(rotation**2, axis=0)),
    ]
    sizes = jnp.concatenate([jnp.stack(sizes), jnp.zeros((128 - len(sizes),), F32)])
    told = gather_small(after(jnp.concatenate([limit, sizes]), *acts_came)).reshape(2, half, -1)
    limits = told[:, :, : limit.shape[0]].astype(BF16)
    acts_came = after(acts_came, cuts, rows_terms[0])
    acts_near = second_step(acts_raw, acts_came)
    acts_away = swap(acts_near, 1)
    mixed_came = after(mixed_came, acts_near, told)
    mixed_near = second_step(mixed_raw, mixed_came)
    mixed_away = swap(mixed_near, 1)
    norms = jnp.sqrt(n * jnp.max(told[:, :, limit.shape[0] :], axis=(0, 1)))
    bound = cot_limit * all_outs**0.5 * (norms[0] * norms[2] + norms[1] * norms[3])
    grad_scale = code_top / jnp.clip(1.02 * bound, 1e-30, 3e38)
    cross_scale = 0.9 / (feat_width**0.5 * jnp.maximum(norms[4], 1e-15))

    shuffle = shuffle[:wide, :wide]
    to_code = grad_scale / jnp.sqrt(F32(all_tokens))

    acts_limit = limits[:, :, :tok_rows].reshape(2, half * tok_rows, 1)
    mixed_limit = limits[:, :, tok_rows:].reshape(2, half * out_block, 1)

    def clip(x, top):
        return jnp.clip(x, -top, top)

    acts_q = [clip(x, top) for x, top in zip((acts_near, acts_away), acts_limit)]
    grad_mixed = sum(dot(x, y, 0, 0) for x, y in zip(cot_owned, acts_q)).astype(BF16)
    mixed_near, mixed_away = after((mixed_near, mixed_away), grad_mixed, rows_terms[1])
    mixed_q = [clip(x, top) for x, top in zip((mixed_near, mixed_away), mixed_limit)]
    grad_acts = sum(
        dot(masked[:, h * half_out : (h + 1) * half_out], mixed_q[h], 1, 0) for h in range(2)
    ).astype(BF16)
    pairs = jnp.concatenate([grad_acts, grad_mixed], axis=0)

    totals, strips = [], []
    for c in range(chunks):
        pair = pairs[:, c * wide : (c + 1) * wide]
        pair = jnp.dot(pair, shuffle, preferred_element_type=F32).astype(BF16)
        away = (dot(pair[:, wide // 2 :], both_plain, 0, 0) * to_code).astype(F16)
        near = dot(pair[:, : wide // 2], both_plain, 0, 0) * to_code
        totals.append(near + swap(away, 1).astype(F32))
    for c in range(chunks):
        total = after(totals[c], *came) if c else totals[c]
        came = scatter_first(total) if n == 8 else ()
        strip = scatter_last(total, came)
        strip = lay_columns(order, strip, jnp.ones((sub, 1), F32), row_block).astype(F16)
        strips.append(strip)

    strip = jnp.concatenate(strips, axis=0)
    blocks = strip.reshape(chunks * sub, n, row_block).transpose(1, 0, 2)
    blocks_way = exchange_steps(blocks)
    blocks = blocks_way.send(blocks_way.send(next(blocks_way)))
    blocks = jnp.concatenate(
        [lax.dynamic_slice_in_dim(blocks, place ^ q, 1, 0) for q in range(n)], axis=0
    )
    gradient = blocks.reshape(n, chunks, sub, row_block).transpose(1, 0, 2, 3)
    unit = 1.0 / grad_scale
    result = after(gradient.reshape(panel, row_block).astype(F32) * unit, strip).T
    factor = -(unit / cross_scale).reshape(1, 1)

    levels = (level + jnp.arange(loops, dtype=jnp.int32)) % loops

    cross_pairs = []
    for c in range(chunks):
        strip = after(strips[c], gradient) if c else strips[c]
        rows = jnp.concatenate(gather_loop(strip), axis=0)
        if c == 0:
            rows, result = after((rows, result), gradient)
        else:
            rows = after(rows, cross_near)
        stacked = jnp.concatenate(split(rows.astype(F32)), axis=0)
        cross = cross_rows(cross_scale.reshape(1, 1), stacked, rot_terms).astype(F16)
        cross_near = second_step(cross, first_step(cross))
        cross_pairs.append((cross_near, swap(cross_near, 1)))
    for c, pair in enumerate(cross_pairs):
        if c:
            pair = after(pair, result)
        terms = [split(x.astype(F32)) for x in pair]
        result = add_product(result, factor, levels, c, rows_terms, terms)
    return result


def solution(mesh):
    in_specs = (P("dp", None), P("dp", None), P(None, "dp"), P("dp", "loop"), P("dp"))
    out_specs = P("dp", "loop")
    return jax.shard_map(
        on_device, mesh=mesh, in_specs=in_specs, out_specs=out_specs, check_vma=False
    )
```

```python
import jax
import jax.numpy as jnp
from jax import lax
from jax.experimental import pallas as pl
from jax.experimental.pallas import tpu as pltpu
from jax.sharding import PartitionSpec as P

clip_ratio = 2.0
eps_power = 1e-06
cot_limit = 6.0
code_top = 30000.0
BF16 = jnp.bfloat16
F16 = jnp.float16
F32 = jnp.float32


def swap(x, mask):
    n = lax.axis_size("dp")
    return lax.ppermute(x, "dp", [(i, i ^ mask) for i in range(n)])


def relative_masks():
    half = lax.axis_size("dp") // 2
    return [(q % half) * 2 + q // half for q in range(2 * half)]


def gather_small(x):
    bit = 1
    while bit < lax.axis_size("dp") // 2:
        x = jnp.concatenate([x, swap(x, 2 * bit)], axis=0)
        bit *= 2
    return jnp.concatenate([x, swap(x, 1)], axis=0)


def tie(*values):
    return lax.optimization_barrier(values)


def first_step(x):
    return (swap(x, 2), swap(x, 4)) if lax.axis_size("dp") == 8 else ()


def after(x, *earlier):
    return lax.optimization_barrier((x,) + earlier)[0]


def far_step(x, came):
    if lax.axis_size("dp") != 8:
        return ()
    half = x.shape[0] // 2
    return swap(came[0][:half], 4), swap(came[1][half:], 2)


def join(x, came, far):
    if lax.axis_size("dp") != 8:
        bit = 1
        while bit < lax.axis_size("dp") // 2:
            x = jnp.concatenate([x, swap(x, 2 * bit)], axis=0)
            bit *= 2
        return x
    return jnp.concatenate([x, *came, *far], axis=0)


def second_step(x, came):
    return join(x, came, far_step(x, came))


def trade(x, mask):
    return swap(x.astype(F16), mask)


def scatter_first(total):
    size = total.shape[0] // (lax.axis_size("dp") // 2)
    far = total[3 * size :]
    half = size // 2
    return trade(far[:half], 2), trade(far[half:], 4)


def scatter_last(total, came):
    chips = lax.axis_size("dp") // 2
    if chips != 4:
        bit = chips // 2
        while bit:
            half = total.shape[0] // 2
            total = total[:half] + trade(total[half:], 2 * bit).astype(F32)
            bit //= 2
        return total
    via_x, via_y = (x.astype(F32) for x in came)
    size = total.shape[0] // chips
    half = size // 2
    own, to_x, to_y = (total[i * size : (i + 1) * size] for i in range(3))
    to_y = jnp.concatenate([to_y[:half] + via_x, to_y[half:]], axis=0)
    to_x = jnp.concatenate([to_x[:half], to_x[half:] + via_y], axis=0)
    return own + trade(to_x, 2).astype(F32) + trade(to_y, 4).astype(F32)


def exchange_steps(x):
    shape = x.shape
    n = shape[0]
    bits = n.bit_length() - 1

    def halve(x, axis):
        stay, go = jnp.split(x, 2, axis=axis)
        return jnp.concatenate([stay, swap(go, 1 if axis == 0 else n >> axis)], axis=axis)

    x = x.reshape((2,) * bits + shape[1:])
    if bits != 3:
        x = yield halve(x, 1)
        for axis in range(2, bits):
            x = halve(x, axis)
    else:
        upper, lower = jnp.split(x, 2, axis=3)
        upper, lower = yield (halve(upper, 1), halve(lower, 2))
        x = jnp.concatenate([halve(upper, 2), halve(lower, 1)], axis=3)
    yield halve(x, 0).reshape(shape)


def gather_loop(x, then=None):
    n = lax.axis_size("loop")

    def turn(r):
        return lax.ppermute(x, "loop", [(i, (i - r) % n) for i in range(n)])

    if n != 4:
        return [x] + [turn(r) for r in range(1, n)]
    me = lax.axis_index("loop")
    after_me, before_me = turn(1), turn(3)
    if then is not None:
        after_me, before_me, then[0] = tie(after_me, before_me, then[0])
    across = jnp.where(me == 1, after_me, jnp.where(me == 2, before_me, x))
    across = lax.ppermute(across, "loop", [(3, 1), (0, 2), (1, 0), (2, 3)])
    return [x, after_me, across, before_me]


def sum_loop(x):
    n = lax.axis_size("loop")
    bit = 1
    while bit < n:
        x = x + lax.ppermute(x, "loop", [(i, i ^ bit) for i in range(n)])
        bit *= 2
    return x


def dot(a, b, ca, cb):
    return lax.dot_general(a, b, (((ca,), (cb,)), ((), ())), preferred_element_type=F32)


def split(x):
    high = lax.reduce_precision(x, 8, 7)
    return high.astype(BF16), (x - high).astype(BF16)


def half_code(x, scale):
    return lax.reduce_precision(x * scale, 5, 10)


def ordered_call(body, order, grid, ins, in_specs, outs, out_specs):
    return pl.pallas_call(
        body,
        out_shape=outs,
        grid_spec=pltpu.PrefetchScalarGridSpec(
            num_scalar_prefetch=1, grid=grid, in_specs=in_specs, out_specs=out_specs
        ),
        compiler_params=pltpu.CompilerParams(vmem_limit_bytes=32 * 1024 * 1024),
    )(order, *ins)


def lay_both(order, tokens, proj_weight, row_block):
    tok_rows, feat_width = tokens.shape
    outs = proj_weight.shape[1]

    def body(order_ref, tok_ref, weight_ref, placed_ref, plain_ref):
        turned = weight_ref[...].T
        for ref in (placed_ref, plain_ref):
            ref[:tok_rows] = tok_ref[...]
            ref[tok_rows:] = turned

    shape = (tok_rows + outs, feat_width)
    block = (tok_rows + outs, row_block)
    return ordered_call(
        body,
        order,
        (feat_width // row_block,),
        (tokens, proj_weight),
        [
            pl.BlockSpec((tok_rows, row_block), lambda q, o: (0, o[q])),
            pl.BlockSpec((row_block, outs), lambda q, o: (o[q], 0)),
        ],
        [jax.ShapeDtypeStruct(shape, BF16)] * 2,
        [pl.BlockSpec(block, lambda q, o: (0, q)), pl.BlockSpec(block, lambda q, o: (0, o[q]))],
    )


def lay_columns(order, x, live, width):
    def body(order_ref, x_ref, live_ref, out_ref):
        out_ref[...] = (x_ref[...].astype(F32) * live_ref[...]).astype(out_ref.dtype)

    rows, cols = x.shape
    return ordered_call(
        body,
        order,
        (cols // width,),
        (x, live),
        [
            pl.BlockSpec((rows, width), lambda q, o: (0, o[q])),
            pl.BlockSpec((rows, 1), lambda q, o: (0, 0)),
        ],
        jax.ShapeDtypeStruct(x.shape, x.dtype),
        pl.BlockSpec((rows, width), lambda q, o: (0, q)),
    )


def plain_call(body, grid, ins, in_specs, out, out_spec, flops, scratch=()):
    size = sum(x.size * x.dtype.itemsize for x in ins) + out.size * out.dtype.itemsize
    return pl.pallas_call(
        body,
        out_shape=out,
        grid=grid,
        in_specs=in_specs,
        out_specs=out_spec,
        scratch_shapes=scratch,
        compiler_params=pltpu.CompilerParams(vmem_limit_bytes=30 * 1024 * 1024),
        cost_estimate=pl.CostEstimate(flops=flops, bytes_accessed=size, transcendentals=0),
    )(*ins)


def cross_rows(scale, stacked, terms):
    (near_high, near_low), (away_high, away_low) = terms
    rows, depth = stacked.shape[0] // 2, stacked.shape[1]
    cols = near_high.shape[1]
    wide = min(cols, 256)
    half = depth // 2

    def body(scale_ref, rows_ref, nh_ref, nl_ref, ah_ref, al_ref, out_ref):
        wide_part = dot(rows_ref[:, :half], nh_ref[...], 1, 0)
        wide_part += dot(rows_ref[:, half:], ah_ref[...], 1, 0)
        total = wide_part[:rows] + wide_part[rows:]
        total += dot(rows_ref[:rows, :half], nl_ref[...], 1, 0)
        total += dot(rows_ref[:rows, half:], al_ref[...], 1, 0)
        out_ref[...] = total * scale_ref[0, 0]

    panel = pl.BlockSpec((half, wide), lambda j: (0, j))
    return plain_call(
        body,
        (cols // wide,),
        (scale, stacked, near_high, near_low, away_high, away_low),
        [
            pl.BlockSpec(memory_space=pltpu.SMEM),
            pl.BlockSpec((2 * rows, depth), lambda j: (0, 0)),
        ]
        + [panel] * 4,
        jax.ShapeDtypeStruct((rows, cols), F32),
        pl.BlockSpec((rows, wide), lambda j: (0, j)),
        6 * rows * depth * cols,
    )


def add_product(base, factor, levels, chunk, rows, terms):
    (near_high, near_low), (away_high, away_low) = terms
    depth, cols = near_high.shape
    height = base.shape[0]
    loops = rows[0].shape[0]
    wide = min(cols, 256)
    places = lax.axis_size("dp") // 2
    part = depth // loops

    def body(factor_ref, level_ref, base_ref, rh_ref, rl_ref, nh_ref, nl_ref, ah_ref, al_ref, out_ref, kept):
        @pl.when(pl.program_id(0) == 0)
        def _():
            for term, ref in enumerate((rh_ref, rl_ref)):
                for r in range(loops):
                    for h in range(2):
                        kept[term, h, :, r * part : (r + 1) * part] = ref[
                            level_ref[r], :, h * part : (h + 1) * part
                        ]

        def by_level(ref):
            x = ref[...].reshape(places, loops, part // places, wide)
            return jnp.concatenate([x[q, r] for r in range(loops) for q in range(places)], axis=0)

        total = 0.0
        for h, (high_ref, low_ref) in enumerate(((nh_ref, nl_ref), (ah_ref, al_ref))):
            high, low = by_level(high_ref), by_level(low_ref)
            total += dot(kept[0, h], high, 1, 0)
            total += dot(kept[1, h], high, 1, 0)
            total += dot(kept[0, h], low, 1, 0)
        out_ref[...] = base_ref[...] + total * factor_ref[0, 0]

    flat = pl.BlockSpec((height, wide), lambda j: (0, j))
    panel = pl.BlockSpec((depth, wide), lambda j: (0, j))
    strip = pl.BlockSpec((loops, height, 2 * part), lambda j: (0, 0, chunk))
    scalars = pl.BlockSpec(memory_space=pltpu.SMEM)
    return plain_call(
        body,
        (cols // wide,),
        (factor, levels, base, *rows, near_high, near_low, away_high, away_low),
        [scalars, scalars, flat, strip, strip] + [panel] * 4,
        jax.ShapeDtypeStruct(base.shape, F32),
        flat,
        12 * height * depth * cols,
        [pltpu.VMEM((2, 2, height, depth), BF16)],
    )


def on_device(tokens, cotangent, proj_weight, rotation, doc_lengths):
    tok_rows, feat_width = tokens.shape
    slot_count = doc_lengths.shape[0]
    slot_len = tok_rows // slot_count
    n, loops = lax.axis_size("dp"), lax.axis_size("loop")
    half = n // 2
    me, level = lax.axis_index("dp"), lax.axis_index("loop")
    place = (me & 1) * half + (me >> 1)
    masks = relative_masks()
    order = jnp.bitwise_xor(me, jnp.array(masks, jnp.int32))
    places = jnp.bitwise_xor(place, jnp.arange(n, dtype=jnp.int32))
    row_block, panel = rotation.shape
    out_block = proj_weight.shape[1]
    all_tokens, all_outs = tok_rows * n, out_block * n
    chunks = max(1, panel // (n * 64))
    wide = panel // chunks
    sub = wide // n

    rot_top = jnp.maximum(jnp.max(jnp.abs(rotation)), 1e-30)
    rot_power = jnp.floor(14.5 - jnp.log2(rot_top))
    rot_scale, rot_unit = jnp.exp2(rot_power), jnp.exp2(-rot_power)
    rot_round = lax.reduce_precision(rotation, 8, 7)
    code = half_code(rotation, rot_scale)
    inner = half_code(rot_round + 0.75 * (rotation - rot_round), rot_scale)
    read = code * rot_unit
    kept = (lax.reduce_precision(read * (1 + 1e-6), 8, 7) == rot_round) & (
        lax.reduce_precision(read * (1 - 1e-6), 8, 7) == rot_round
    )
    rot_code = jnp.where(kept, code, inner).astype(F16)
    rot_units = jnp.full((128,), rot_unit)
    bit = 1
    while bit < half:
        rot_units = jnp.concatenate([rot_units, swap(rot_units, 2 * bit)], axis=0)
        bit *= 2
    rot_code, rot_units = tie(rot_code, rot_units)
    rot_units = jnp.concatenate([rot_units, swap(rot_units, 1)], axis=0)
    rot_units = rot_units.reshape(2, half, 1, 128)[:, :, :, :1]
    tokens, cotangent, proj_weight, rot_code = tie(tokens, cotangent, proj_weight, rot_code)
    rot_came = first_step(rot_code)

    def decode(part, units):
        part = part.reshape(half, row_block, panel).astype(F32) * units
        return split(part.reshape(half * row_block, panel))

    positions = jnp.arange(tok_rows, dtype=jnp.int32)
    slot_match = (positions // slot_len)[:, None] == jnp.arange(slot_count, dtype=jnp.int32)[
        None, :
    ]
    row_lengths = jnp.sum(jnp.where(slot_match, doc_lengths[None, :], 0), axis=1)
    live_rows = positions % slot_len < row_lengths
    masked = lay_columns(order, cotangent, live_rows.astype(F32)[:, None], out_block)
    both, both_plain = lay_both(order, tokens, proj_weight, row_block)
    cuts = masked.reshape(tok_rows, n, out_block).transpose(1, 0, 2)
    cols = jnp.arange(panel, dtype=jnp.int32)
    source = cols - cols % wide + (((cols % wide) // sub) ^ place) * sub + cols % sub
    shuffle = (cols[:, None] == source[None, :]).astype(BF16)
    rows_terms = [
        dot(x, shuffle, 1, 0).astype(BF16) for x in split(tie(rotation, tokens)[0])
    ]
    rows_sent = rows_terms
    rot_came, cuts, rows_terms, rot_units = tie(rot_came, cuts, rows_terms, rot_units)
    rows_terms = [lax.all_gather(x, "loop", axis=0) for x in rows_sent]
    rot_far = far_step(rot_code, rot_came)
    rot_far, both, both_plain = tie(rot_far, both, both_plain)
    rot_near = join(rot_code, rot_came, rot_far)
    rot_away = swap(rot_near, 1)
    cuts_way = exchange_steps(cuts)
    cuts = next(cuts_way)
    rot_terms = [decode(rot_near, rot_units[0])]
    near_part = dot(both[:, : feat_width // 2], rot_terms[0][0], 1, 0)

    half_feat, half_out = feat_width // 2, all_outs // 2
    rot_away, near_part, cuts = tie(rot_away, near_part, cuts)
    rot_terms.append(decode(rot_away, rot_units[1]))
    cuts = cuts_way.send(cuts)
    rotated = near_part + dot(both[:, half_feat:], rot_terms[1][0], 1, 0)
    acts_raw, mixed_raw = rotated[:tok_rows].astype(BF16), rotated[tok_rows:].astype(BF16)
    power = after(jnp.sum(rotated * rotated, axis=1), acts_raw, mixed_raw)
    acts_came = first_step(acts_raw)
    acts_came, mixed_raw = tie(acts_came, mixed_raw)
    mixed_came = first_step(mixed_raw)
    power = sum_loop(power)
    tokens, proj_weight, rotation = after((tokens, proj_weight, rotation), acts_raw)
    limit = clip_ratio * jnp.sqrt(power / feat_width + eps_power)
    tok_top = jnp.max(jnp.abs(tokens), axis=1).astype(F32)
    weight_top = jnp.max(jnp.abs(proj_weight), axis=0).astype(F32)
    sizes = [
        jnp.sum(limit[tok_rows:] ** 2),
        jnp.sum(limit[:tok_rows] ** 2),
        jnp.sum(tok_top**2),
        jnp.sum(weight_top**2),
        jnp.max(jnp.sum(rotation**2, axis=0)),
    ]
    sizes = jnp.concatenate([jnp.stack(sizes), jnp.zeros((128 - len(sizes),), F32)])
    acts_came, rows_high = tie(acts_came, rows_terms[0])
    rows_terms = [rows_high, rows_terms[1]]
    acts_far = far_step(acts_raw, acts_came)
    told = jnp.concatenate([limit, sizes])
    acts_far, told, cuts = tie(acts_far, told, cuts)
    acts_near = join(acts_raw, acts_came, acts_far)
    acts_away = swap(acts_near, 1)
    told = gather_small(told)
    cot_owned = cuts.reshape(2, half * tok_rows, out_block)
    mixed_near = second_step(mixed_raw, mixed_came)
    mixed_near, told = tie(mixed_near, told)
    told = told.reshape(2, half, -1)
    mixed_away = swap(mixed_near, 1)
    limits = told[:, :, : limit.shape[0]].astype(BF16)
    norms = jnp.sqrt(n * jnp.max(told[:, :, limit.shape[0] :], axis=(0, 1)))
    bound = cot_limit * all_outs**0.5 * (norms[0] * norms[2] + norms[1] * norms[3])
    grad_scale = code_top / jnp.clip(1.02 * bound, 1e-30, 3e38)
    cross_scale = 0.9 / (feat_width**0.5 * jnp.maximum(norms[4], 1e-15))

    shuffle = shuffle[:wide, :wide]
    to_code = grad_scale / jnp.sqrt(F32(all_tokens))

    acts_limit = limits[:, :, :tok_rows].reshape(2, half * tok_rows, 1)
    mixed_limit = limits[:, :, tok_rows:].reshape(2, half * out_block, 1)

    def clip(x, top):
        return jnp.clip(x, -top, top)

    acts_q = [clip(x, top) for x, top in zip((acts_near, acts_away), acts_limit)]
    grad_mixed = sum(dot(x, y, 0, 0) for x, y in zip(cot_owned, acts_q)).astype(BF16)
    mixed_near, mixed_away, grad_mixed, rows_low = tie(
        mixed_near, mixed_away, grad_mixed, rows_terms[1]
    )
    rows_terms = [rows_terms[0], rows_low]
    mixed_q = [clip(x, top) for x, top in zip((mixed_near, mixed_away), mixed_limit)]
    grad_acts = sum(
        dot(masked[:, h * half_out : (h + 1) * half_out], mixed_q[h], 1, 0) for h in range(2)
    ).astype(BF16)
    pairs = jnp.concatenate([grad_acts, grad_mixed], axis=0)

    totals, strips = [], []
    for c in range(chunks):
        pair = pairs[:, c * wide : (c + 1) * wide]
        pair = jnp.dot(pair, shuffle, preferred_element_type=F32).astype(BF16)
        away = (dot(pair[:, wide // 2 :], both_plain, 0, 0) * to_code).astype(F16)
        near = dot(pair[:, : wide // 2], both_plain, 0, 0) * to_code
        totals.append(near + swap(away, 1).astype(F32))
    for c in range(chunks):
        came = scatter_first(totals[c]) if n == 8 else ()
        if c + 1 < chunks:
            totals[c + 1], came = tie(totals[c + 1], came)
        strip = scatter_last(totals[c], came)
        strip = lay_columns(order, strip, jnp.ones((sub, 1), F32), row_block).astype(F16)
        strips.append(strip)

    strip = jnp.concatenate(strips, axis=0)
    blocks = strip.reshape(chunks * sub, n, row_block).transpose(1, 0, 2)
    blocks_way = exchange_steps(blocks)
    blocks = blocks_way.send(next(blocks_way))
    blocks = jnp.concatenate(
        [lax.dynamic_slice_in_dim(blocks, place ^ q, 1, 0) for q in range(n)], axis=0
    )
    gradient = blocks.reshape(n, chunks, sub, row_block).transpose(1, 0, 2, 3)
    unit = 1.0 / grad_scale
    gradient = lax.optimization_barrier(gradient.reshape(panel, row_block).astype(F32) * unit)
    result = gradient.T
    factor = -(unit / cross_scale).reshape(1, 1)

    levels = (level + jnp.arange(loops, dtype=jnp.int32)) % loops

    cross_pairs = []
    for c in range(chunks):
        later = strips[c + 1 : c + 2]
        rows = jnp.concatenate(gather_loop(strips[c], later or None), axis=0)
        strips[c + 1 : c + 2] = later
        if c:
            rows, cross_near = tie(rows, cross_near)
            cross_pairs.append((cross_near, swap(cross_near, 1)))
        else:
            rows, result = tie(rows, result)
        stacked = jnp.concatenate(split(rows.astype(F32)), axis=0)
        cross = cross_rows(cross_scale.reshape(1, 1), stacked, rot_terms).astype(F16)
        came = first_step(cross)
        if c + 1 < chunks:
            cross_near = second_step(cross, came)
    for c, pair in enumerate(cross_pairs):
        result = add_product(result, factor, levels, c, rows_terms, [split(x.astype(F32)) for x in pair])
    far = far_step(cross, came)
    far, result = tie(far, result)
    cross_near = join(cross, came, far)
    pair = (cross_near, swap(cross_near, 1))
    terms = [split(x.astype(F32)) for x in pair]
    result = add_product(result, factor, levels, chunks - 1, rows_terms, terms)
    return result


def solution(mesh):
    in_specs = (P("dp", None), P("dp", None), P(None, "dp"), P("dp", "loop"), P("dp"))
    out_specs = P("dp", "loop")
    return jax.shard_map(
        on_device, mesh=mesh, in_specs=in_specs, out_specs=out_specs, check_vma=False
    )
```

```python
import jax
import jax.numpy as jnp
from jax import lax
from jax.experimental import pallas as pl
from jax.experimental.pallas import tpu as pltpu
from jax.sharding import PartitionSpec as P

clip_ratio = 2.0
eps_power = 1e-06
cot_limit = 6.0
code_top = 30000.0
BF16 = jnp.bfloat16
F16 = jnp.float16
F32 = jnp.float32


def swap(x, mask):
    n = lax.axis_size("dp")
    return lax.ppermute(x, "dp", [(i, i ^ mask) for i in range(n)])


def relative_masks():
    half = lax.axis_size("dp") // 2
    return [(q % half) * 2 + q // half for q in range(2 * half)]


def gather_small(x):
    bit = 1
    while bit < lax.axis_size("dp") // 2:
        x = jnp.concatenate([x, swap(x, 2 * bit)], axis=0)
        bit *= 2
    return jnp.concatenate([x, swap(x, 1)], axis=0)


def tie(*values):
    return lax.optimization_barrier(values)


def first_step(x):
    return (swap(x, 2), swap(x, 4)) if lax.axis_size("dp") == 8 else ()


def after(x, *earlier):
    return lax.optimization_barrier((x,) + earlier)[0]


def far_step(x, came):
    if lax.axis_size("dp") != 8:
        return ()
    half = x.shape[0] // 2
    return swap(came[0][:half], 4), swap(came[1][half:], 2)


def join(x, came, far):
    if lax.axis_size("dp") != 8:
        bit = 1
        while bit < lax.axis_size("dp") // 2:
            x = jnp.concatenate([x, swap(x, 2 * bit)], axis=0)
            bit *= 2
        return x
    return jnp.concatenate([x, *came, *far], axis=0)


def second_step(x, came):
    return join(x, came, far_step(x, came))


def trade(x, mask):
    return swap(x.astype(F16), mask)


def scatter_first(total):
    size = total.shape[0] // (lax.axis_size("dp") // 2)
    far = total[3 * size :]
    half = size // 2
    return trade(far[:half], 2), trade(far[half:], 4)


def scatter_last(total, came):
    chips = lax.axis_size("dp") // 2
    if chips != 4:
        bit = chips // 2
        while bit:
            half = total.shape[0] // 2
            total = total[:half] + trade(total[half:], 2 * bit).astype(F32)
            bit //= 2
        return total
    via_x, via_y = (x.astype(F32) for x in came)
    size = total.shape[0] // chips
    half = size // 2
    own, to_x, to_y = (total[i * size : (i + 1) * size] for i in range(3))
    to_y = jnp.concatenate([to_y[:half] + via_x, to_y[half:]], axis=0)
    to_x = jnp.concatenate([to_x[:half], to_x[half:] + via_y], axis=0)
    return own + trade(to_x, 2).astype(F32) + trade(to_y, 4).astype(F32)


def exchange_steps(x):
    shape = x.shape
    n = shape[0]
    bits = n.bit_length() - 1

    def halve(x, axis):
        stay, go = jnp.split(x, 2, axis=axis)
        return jnp.concatenate([stay, swap(go, 1 if axis == 0 else n >> axis)], axis=axis)

    x = x.reshape((2,) * bits + shape[1:])
    if bits != 3:
        x = yield halve(x, 1)
        for axis in range(2, bits):
            x = halve(x, axis)
    else:
        upper, lower = jnp.split(x, 2, axis=3)
        upper, lower = yield (halve(upper, 1), halve(lower, 2))
        x = jnp.concatenate([halve(upper, 2), halve(lower, 1)], axis=3)
    yield halve(x, 0).reshape(shape)


def gather_loop(x, then=None):
    n = lax.axis_size("loop")

    def turn(r):
        return lax.ppermute(x, "loop", [(i, (i - r) % n) for i in range(n)])

    if n != 4:
        return [x] + [turn(r) for r in range(1, n)]
    me = lax.axis_index("loop")
    after_me, before_me = turn(1), turn(3)
    if then is not None:
        after_me, before_me, then[0] = tie(after_me, before_me, then[0])
    across = jnp.where(me == 1, after_me, jnp.where(me == 2, before_me, x))
    across = lax.ppermute(across, "loop", [(3, 1), (0, 2), (1, 0), (2, 3)])
    return [x, after_me, across, before_me]


def sum_loop(x):
    n = lax.axis_size("loop")
    bit = 1
    while bit < n:
        x = x + lax.ppermute(x, "loop", [(i, i ^ bit) for i in range(n)])
        bit *= 2
    return x


def dot(a, b, ca, cb):
    return lax.dot_general(a, b, (((ca,), (cb,)), ((), ())), preferred_element_type=F32)


def split(x):
    high = lax.reduce_precision(x, 8, 7)
    return high.astype(BF16), (x - high).astype(BF16)


def half_code(x, scale):
    return lax.reduce_precision(x * scale, 5, 10)


def ordered_call(body, order, grid, ins, in_specs, outs, out_specs):
    return pl.pallas_call(
        body,
        out_shape=outs,
        grid_spec=pltpu.PrefetchScalarGridSpec(
            num_scalar_prefetch=1, grid=grid, in_specs=in_specs, out_specs=out_specs
        ),
        compiler_params=pltpu.CompilerParams(vmem_limit_bytes=32 * 1024 * 1024),
    )(order, *ins)


def lay_both(order, tokens, proj_weight, row_block):
    tok_rows, feat_width = tokens.shape
    outs = proj_weight.shape[1]

    def body(order_ref, tok_ref, weight_ref, placed_ref, plain_ref):
        turned = weight_ref[...].T
        for ref in (placed_ref, plain_ref):
            ref[:tok_rows] = tok_ref[...]
            ref[tok_rows:] = turned

    shape = (tok_rows + outs, feat_width)
    block = (tok_rows + outs, row_block)
    return ordered_call(
        body,
        order,
        (feat_width // row_block,),
        (tokens, proj_weight),
        [
            pl.BlockSpec((tok_rows, row_block), lambda q, o: (0, o[q])),
            pl.BlockSpec((row_block, outs), lambda q, o: (o[q], 0)),
        ],
        [jax.ShapeDtypeStruct(shape, BF16)] * 2,
        [pl.BlockSpec(block, lambda q, o: (0, q)), pl.BlockSpec(block, lambda q, o: (0, o[q]))],
    )


def lay_columns(order, x, live, width):
    def body(order_ref, x_ref, live_ref, out_ref):
        out_ref[...] = (x_ref[...].astype(F32) * live_ref[...]).astype(out_ref.dtype)

    rows, cols = x.shape
    return ordered_call(
        body,
        order,
        (cols // width,),
        (x, live),
        [
            pl.BlockSpec((rows, width), lambda q, o: (0, o[q])),
            pl.BlockSpec((rows, 1), lambda q, o: (0, 0)),
        ],
        jax.ShapeDtypeStruct(x.shape, x.dtype),
        pl.BlockSpec((rows, width), lambda q, o: (0, q)),
    )


def plain_call(body, grid, ins, in_specs, out, out_spec, flops, scratch=()):
    size = sum(x.size * x.dtype.itemsize for x in ins) + out.size * out.dtype.itemsize
    return pl.pallas_call(
        body,
        out_shape=out,
        grid=grid,
        in_specs=in_specs,
        out_specs=out_spec,
        scratch_shapes=scratch,
        compiler_params=pltpu.CompilerParams(vmem_limit_bytes=30 * 1024 * 1024),
        cost_estimate=pl.CostEstimate(flops=flops, bytes_accessed=size, transcendentals=0),
    )(*ins)


def cross_rows(scale, stacked, terms):
    (near_high, near_low), (away_high, away_low) = terms
    rows, depth = stacked.shape[0] // 2, stacked.shape[1]
    cols = near_high.shape[1]
    wide = min(cols, 256)
    half = depth // 2

    def body(scale_ref, rows_ref, nh_ref, nl_ref, ah_ref, al_ref, out_ref):
        wide_part = dot(rows_ref[:, :half], nh_ref[...], 1, 0)
        wide_part += dot(rows_ref[:, half:], ah_ref[...], 1, 0)
        total = wide_part[:rows] + wide_part[rows:]
        total += dot(rows_ref[:rows, :half], nl_ref[...], 1, 0)
        total += dot(rows_ref[:rows, half:], al_ref[...], 1, 0)
        out_ref[...] = total * scale_ref[0, 0]

    panel = pl.BlockSpec((half, wide), lambda j: (0, j))
    return plain_call(
        body,
        (cols // wide,),
        (scale, stacked, near_high, near_low, away_high, away_low),
        [
            pl.BlockSpec(memory_space=pltpu.SMEM),
            pl.BlockSpec((2 * rows, depth), lambda j: (0, 0)),
        ]
        + [panel] * 4,
        jax.ShapeDtypeStruct((rows, cols), F32),
        pl.BlockSpec((rows, wide), lambda j: (0, j)),
        6 * rows * depth * cols,
    )


def add_product(base, factor, levels, chunk, rows, terms):
    (near_high, near_low), (away_high, away_low) = terms
    depth, cols = near_high.shape
    height = base.shape[0]
    loops = rows[0].shape[0]
    wide = min(cols, 256)
    places = lax.axis_size("dp") // 2
    part = depth // loops

    def body(factor_ref, level_ref, base_ref, rh_ref, rl_ref, nh_ref, nl_ref, ah_ref, al_ref, out_ref, kept):
        @pl.when(pl.program_id(0) == 0)
        def _():
            for term, ref in enumerate((rh_ref, rl_ref)):
                for r in range(loops):
                    for h in range(2):
                        kept[term, h, :, r * part : (r + 1) * part] = ref[
                            level_ref[r], :, h * part : (h + 1) * part
                        ]

        def by_level(ref):
            x = ref[...].reshape(places, loops, part // places, wide)
            return jnp.concatenate([x[q, r] for r in range(loops) for q in range(places)], axis=0)

        total = 0.0
        for h, (high_ref, low_ref) in enumerate(((nh_ref, nl_ref), (ah_ref, al_ref))):
            high, low = by_level(high_ref), by_level(low_ref)
            total += dot(kept[0, h], high, 1, 0)
            total += dot(kept[1, h], high, 1, 0)
            total += dot(kept[0, h], low, 1, 0)
        out_ref[...] = base_ref[...] + total * factor_ref[0, 0]

    flat = pl.BlockSpec((height, wide), lambda j: (0, j))
    panel = pl.BlockSpec((depth, wide), lambda j: (0, j))
    strip = pl.BlockSpec((loops, height, 2 * part), lambda j: (0, 0, chunk))
    scalars = pl.BlockSpec(memory_space=pltpu.SMEM)
    return plain_call(
        body,
        (cols // wide,),
        (factor, levels, base, *rows, near_high, near_low, away_high, away_low),
        [scalars, scalars, flat, strip, strip] + [panel] * 4,
        jax.ShapeDtypeStruct(base.shape, F32),
        flat,
        12 * height * depth * cols,
        [pltpu.VMEM((2, 2, height, depth), BF16)],
    )


def on_device(tokens, cotangent, proj_weight, rotation, doc_lengths):
    tok_rows, feat_width = tokens.shape
    slot_count = doc_lengths.shape[0]
    slot_len = tok_rows // slot_count
    n, loops = lax.axis_size("dp"), lax.axis_size("loop")
    half = n // 2
    me, level = lax.axis_index("dp"), lax.axis_index("loop")
    place = (me & 1) * half + (me >> 1)
    masks = relative_masks()
    order = jnp.bitwise_xor(me, jnp.array(masks, jnp.int32))
    places = jnp.bitwise_xor(place, jnp.arange(n, dtype=jnp.int32))
    row_block, panel = rotation.shape
    out_block = proj_weight.shape[1]
    all_tokens, all_outs = tok_rows * n, out_block * n
    chunks = max(1, panel // (n * 64))
    wide = panel // chunks
    sub = wide // n

    rot_top = jnp.maximum(jnp.max(jnp.abs(rotation)), 1e-30)
    rot_power = jnp.floor(14.5 - jnp.log2(rot_top))
    rot_scale, rot_unit = jnp.exp2(rot_power), jnp.exp2(-rot_power)
    rot_round = lax.reduce_precision(rotation, 8, 7)
    code = half_code(rotation, rot_scale)
    inner = half_code(rot_round + 0.75 * (rotation - rot_round), rot_scale)
    read = code * rot_unit
    kept = (lax.reduce_precision(read * (1 + 1e-6), 8, 7) == rot_round) & (
        lax.reduce_precision(read * (1 - 1e-6), 8, 7) == rot_round
    )
    rot_code = jnp.where(kept, code, inner).astype(F16)
    rot_units = jnp.full((128,), rot_unit)
    bit = 1
    while bit < half:
        rot_units = jnp.concatenate([rot_units, swap(rot_units, 2 * bit)], axis=0)
        bit *= 2
    rot_code, rot_units = tie(rot_code, rot_units)
    rot_units = jnp.concatenate([rot_units, swap(rot_units, 1)], axis=0)
    rot_units = rot_units.reshape(2, half, 1, 128)[:, :, :, :1]
    tokens, cotangent, proj_weight, rot_code = tie(tokens, cotangent, proj_weight, rot_code)
    rot_came = first_step(rot_code)

    def decode(part, units):
        part = part.reshape(half, row_block, panel).astype(F32) * units
        return split(part.reshape(half * row_block, panel))

    positions = jnp.arange(tok_rows, dtype=jnp.int32)
    slot_match = (positions // slot_len)[:, None] == jnp.arange(slot_count, dtype=jnp.int32)[
        None, :
    ]
    row_lengths = jnp.sum(jnp.where(slot_match, doc_lengths[None, :], 0), axis=1)
    live_rows = positions % slot_len < row_lengths
    masked = lay_columns(order, cotangent, live_rows.astype(F32)[:, None], out_block)
    both, both_plain = lay_both(order, tokens, proj_weight, row_block)
    cuts = masked.reshape(tok_rows, n, out_block).transpose(1, 0, 2)
    cols = jnp.arange(panel, dtype=jnp.int32)
    source = cols - cols % wide + (((cols % wide) // sub) ^ place) * sub + cols % sub
    shuffle = (cols[:, None] == source[None, :]).astype(BF16)
    rows_terms = [
        dot(x, shuffle, 1, 0).astype(BF16) for x in split(tie(rotation, tokens)[0])
    ]
    rows_sent = rows_terms
    rot_came, cuts, rows_terms, rot_units = tie(rot_came, cuts, rows_terms, rot_units)
    rows_terms = [lax.all_gather(x, "loop", axis=0) for x in rows_sent]
    rot_far = far_step(rot_code, rot_came)
    rot_far, both, both_plain = tie(rot_far, both, both_plain)
    rot_near = join(rot_code, rot_came, rot_far)
    rot_away = swap(rot_near, 1)
    cuts_way = exchange_steps(cuts)
    cuts = next(cuts_way)
    rot_terms = [decode(rot_near, rot_units[0])]
    near_part = dot(both[:, : feat_width // 2], rot_terms[0][0], 1, 0)

    half_feat, half_out = feat_width // 2, all_outs // 2
    rot_away, near_part, cuts = tie(rot_away, near_part, cuts)
    rot_terms.append(decode(rot_away, rot_units[1]))
    cuts = cuts_way.send(cuts)
    rotated = near_part + dot(both[:, half_feat:], rot_terms[1][0], 1, 0)
    acts_raw, mixed_raw = rotated[:tok_rows].astype(BF16), rotated[tok_rows:].astype(BF16)
    power = after(jnp.sum(rotated * rotated, axis=1), acts_raw, mixed_raw)
    acts_came = first_step(acts_raw)
    acts_came, mixed_raw = tie(acts_came, mixed_raw)
    mixed_came = first_step(mixed_raw)
    power = sum_loop(power)
    tokens, proj_weight, rotation = after((tokens, proj_weight, rotation), acts_raw)
    limit = clip_ratio * jnp.sqrt(power / feat_width + eps_power)
    tok_top = jnp.max(jnp.abs(tokens), axis=1).astype(F32)
    weight_top = jnp.max(jnp.abs(proj_weight), axis=0).astype(F32)
    sizes = [
        jnp.sum(limit[tok_rows:] ** 2),
        jnp.sum(limit[:tok_rows] ** 2),
        jnp.sum(tok_top**2),
        jnp.sum(weight_top**2),
        jnp.max(jnp.sum(rotation**2, axis=0)),
    ]
    sizes = jnp.concatenate([jnp.stack(sizes), jnp.zeros((128 - len(sizes),), F32)])
    acts_came, rows_high = tie(acts_came, rows_terms[0])
    rows_terms = [rows_high, rows_terms[1]]
    acts_far = far_step(acts_raw, acts_came)
    told = jnp.concatenate([limit, sizes])
    acts_far, told, cuts = tie(acts_far, told, cuts)
    acts_near = join(acts_raw, acts_came, acts_far)
    acts_away = swap(acts_near, 1)
    told = gather_small(told)
    cot_owned = cuts.reshape(2, half * tok_rows, out_block)
    mixed_near = second_step(mixed_raw, mixed_came)
    mixed_near, told = tie(mixed_near, told)
    told = told.reshape(2, half, -1)
    mixed_away = swap(mixed_near, 1)
    limits = told[:, :, : limit.shape[0]].astype(BF16)
    norms = jnp.sqrt(n * jnp.max(told[:, :, limit.shape[0] :], axis=(0, 1)))
    bound = cot_limit * all_outs**0.5 * (norms[0] * norms[2] + norms[1] * norms[3])
    grad_scale = code_top / jnp.clip(1.02 * bound, 1e-30, 3e38)
    cross_scale = 0.9 / (feat_width**0.5 * jnp.maximum(norms[4], 1e-15))

    shuffle = shuffle[:wide, :wide]
    to_code = grad_scale / jnp.sqrt(F32(all_tokens))

    acts_limit = limits[:, :, :tok_rows].reshape(2, half * tok_rows, 1)
    mixed_limit = limits[:, :, tok_rows:].reshape(2, half * out_block, 1)

    def clip(x, top):
        return jnp.clip(x, -top, top)

    acts_q = [clip(x, top) for x, top in zip((acts_near, acts_away), acts_limit)]
    grad_mixed = sum(dot(x, y, 0, 0) for x, y in zip(cot_owned, acts_q)).astype(BF16)
    mixed_near, mixed_away, grad_mixed, rows_low = tie(
        mixed_near, mixed_away, grad_mixed, rows_terms[1]
    )
    rows_terms = [rows_terms[0], rows_low]
    mixed_q = [clip(x, top) for x, top in zip((mixed_near, mixed_away), mixed_limit)]
    grad_acts = sum(
        dot(masked[:, h * half_out : (h + 1) * half_out], mixed_q[h], 1, 0) for h in range(2)
    ).astype(BF16)
    pairs = jnp.concatenate([grad_acts, grad_mixed], axis=0)

    totals, strips = [], []
    for c in range(chunks):
        pair = pairs[:, c * wide : (c + 1) * wide]
        pair = jnp.dot(pair, shuffle, preferred_element_type=F32).astype(BF16)
        away = (dot(pair[:, wide // 2 :], both_plain, 0, 0) * to_code).astype(F16)
        near = dot(pair[:, : wide // 2], both_plain, 0, 0) * to_code
        totals.append(near + swap(away, 1).astype(F32))
    for c in range(chunks):
        came = scatter_first(totals[c]) if n == 8 else ()
        if c + 1 < chunks:
            totals[c + 1], came = tie(totals[c + 1], came)
        strip = scatter_last(totals[c], came)
        strip = lay_columns(order, strip, jnp.ones((sub, 1), F32), row_block).astype(F16)
        strips.append(strip)

    strip = jnp.concatenate(strips, axis=0)
    blocks = strip.reshape(chunks * sub, n, row_block).transpose(1, 0, 2)
    blocks_way = exchange_steps(blocks)
    blocks = blocks_way.send(next(blocks_way))
    blocks = jnp.concatenate(
        [lax.dynamic_slice_in_dim(blocks, place ^ q, 1, 0) for q in range(n)], axis=0
    )
    gradient = blocks.reshape(n, chunks, sub, row_block).transpose(1, 0, 2, 3)
    unit = 1.0 / grad_scale
    gradient = lax.optimization_barrier(gradient.reshape(panel, row_block).astype(F32) * unit)
    result = gradient.T
    factor = -(unit / cross_scale).reshape(1, 1)

    levels = (level + jnp.arange(loops, dtype=jnp.int32)) % loops

    cross_pairs = []
    for c in range(chunks):
        later = strips[c + 1 : c + 2]
        rows = jnp.concatenate(gather_loop(strips[c], later or None), axis=0)
        strips[c + 1 : c + 2] = later
        if c:
            rows, cross_near = tie(rows, cross_near)
            cross_pairs.append((cross_near, swap(cross_near, 1)))
        else:
            rows, result = tie(rows, result)
        stacked = jnp.concatenate(split(rows.astype(F32)), axis=0)
        cross = cross_rows(cross_scale.reshape(1, 1), stacked, rot_terms).astype(F16)
        came = first_step(cross)
        if c + 1 < chunks:
            cross_near = second_step(cross, came)
    for c, pair in enumerate(cross_pairs):
        result = add_product(result, factor, levels, c, rows_terms, [split(x.astype(F32)) for x in pair])
    came, result = tie(came, result)
    far = far_step(cross, came)
    cross_near = join(cross, came, far)
    pair = (cross_near, swap(cross_near, 1))
    terms = [split(x.astype(F32)) for x in pair]
    result = add_product(result, factor, levels, chunks - 1, rows_terms, terms)
    return result


def solution(mesh):
    in_specs = (P("dp", None), P("dp", None), P(None, "dp"), P("dp", "loop"), P("dp"))
    out_specs = P("dp", "loop")
    return jax.shard_map(
        on_device, mesh=mesh, in_specs=in_specs, out_specs=out_specs, check_vma=False
    )
```

```python
import jax
import jax.numpy as jnp
from jax import lax
from jax.experimental import pallas as pl
from jax.experimental.pallas import tpu as pltpu
from jax.sharding import PartitionSpec as P

clip_ratio = 2.0
eps_power = 1e-06
cot_limit = 6.0
code_top = 30000.0
BF16 = jnp.bfloat16
F16 = jnp.float16
F32 = jnp.float32


def swap(x, mask):
    n = lax.axis_size("dp")
    return lax.ppermute(x, "dp", [(i, i ^ mask) for i in range(n)])


def relative_masks():
    half = lax.axis_size("dp") // 2
    return [(q % half) * 2 + q // half for q in range(2 * half)]


def gather_small(x):
    bit = 1
    while bit < lax.axis_size("dp") // 2:
        x = jnp.concatenate([x, swap(x, 2 * bit)], axis=0)
        bit *= 2
    return jnp.concatenate([x, swap(x, 1)], axis=0)


def tie(*values):
    return lax.optimization_barrier(values)


def first_step(x):
    return (swap(x, 2), swap(x, 4)) if lax.axis_size("dp") == 8 else ()


def after(x, *earlier):
    return lax.optimization_barrier((x,) + earlier)[0]


def far_step(x, came):
    if lax.axis_size("dp") != 8:
        return ()
    half = x.shape[0] // 2
    return swap(came[0][:half], 4), swap(came[1][half:], 2)


def join(x, came, far):
    if lax.axis_size("dp") != 8:
        bit = 1
        while bit < lax.axis_size("dp") // 2:
            x = jnp.concatenate([x, swap(x, 2 * bit)], axis=0)
            bit *= 2
        return x
    return jnp.concatenate([x, *came, *far], axis=0)


def second_step(x, came):
    return join(x, came, far_step(x, came))


def trade(x, mask):
    return swap(x.astype(F16), mask)


def scatter_first(total):
    size = total.shape[0] // (lax.axis_size("dp") // 2)
    far = total[3 * size :]
    half = size // 2
    return trade(far[:half], 2), trade(far[half:], 4)


def scatter_last(total, came):
    chips = lax.axis_size("dp") // 2
    if chips != 4:
        bit = chips // 2
        while bit:
            half = total.shape[0] // 2
            total = total[:half] + trade(total[half:], 2 * bit).astype(F32)
            bit //= 2
        return total
    via_x, via_y = (x.astype(F32) for x in came)
    size = total.shape[0] // chips
    half = size // 2
    own, to_x, to_y = (total[i * size : (i + 1) * size] for i in range(3))
    to_y = jnp.concatenate([to_y[:half] + via_x, to_y[half:]], axis=0)
    to_x = jnp.concatenate([to_x[:half], to_x[half:] + via_y], axis=0)
    return own + trade(to_x, 2).astype(F32) + trade(to_y, 4).astype(F32)


def exchange_steps(x):
    shape = x.shape
    n = shape[0]
    bits = n.bit_length() - 1

    def halve(x, axis):
        stay, go = jnp.split(x, 2, axis=axis)
        return jnp.concatenate([stay, swap(go, 1 if axis == 0 else n >> axis)], axis=axis)

    x = x.reshape((2,) * bits + shape[1:])
    if bits != 3:
        x = yield halve(x, 1)
        for axis in range(2, bits):
            x = halve(x, axis)
    else:
        upper, lower = jnp.split(x, 2, axis=3)
        upper, lower = yield (halve(upper, 1), halve(lower, 2))
        x = jnp.concatenate([halve(upper, 2), halve(lower, 1)], axis=3)
    yield halve(x, 0).reshape(shape)


def gather_loop(x, then=None):
    n = lax.axis_size("loop")

    def turn(r):
        return lax.ppermute(x, "loop", [(i, (i - r) % n) for i in range(n)])

    if n != 4:
        return [x] + [turn(r) for r in range(1, n)]
    me = lax.axis_index("loop")
    after_me, before_me = turn(1), turn(3)
    if then is not None:
        after_me, before_me, then[0] = tie(after_me, before_me, then[0])
    across = jnp.where(me == 1, after_me, jnp.where(me == 2, before_me, x))
    across = lax.ppermute(across, "loop", [(3, 1), (0, 2), (1, 0), (2, 3)])
    return [x, after_me, across, before_me]


def sum_loop(x):
    n = lax.axis_size("loop")
    bit = 1
    while bit < n:
        x = x + lax.ppermute(x, "loop", [(i, i ^ bit) for i in range(n)])
        bit *= 2
    return x


def dot(a, b, ca, cb):
    return lax.dot_general(a, b, (((ca,), (cb,)), ((), ())), preferred_element_type=F32)


def split(x):
    high = lax.reduce_precision(x, 8, 7)
    return high.astype(BF16), (x - high).astype(BF16)


def half_code(x, scale):
    return lax.reduce_precision(x * scale, 5, 10)


def ordered_call(body, order, grid, ins, in_specs, outs, out_specs):
    return pl.pallas_call(
        body,
        out_shape=outs,
        grid_spec=pltpu.PrefetchScalarGridSpec(
            num_scalar_prefetch=1, grid=grid, in_specs=in_specs, out_specs=out_specs
        ),
        compiler_params=pltpu.CompilerParams(vmem_limit_bytes=32 * 1024 * 1024),
    )(order, *ins)


def lay_both(order, tokens, proj_weight, row_block):
    tok_rows, feat_width = tokens.shape
    outs = proj_weight.shape[1]

    def body(order_ref, tok_ref, weight_ref, placed_ref, plain_ref):
        turned = weight_ref[...].T
        for ref in (placed_ref, plain_ref):
            ref[:tok_rows] = tok_ref[...]
            ref[tok_rows:] = turned

    shape = (tok_rows + outs, feat_width)
    block = (tok_rows + outs, row_block)
    return ordered_call(
        body,
        order,
        (feat_width // row_block,),
        (tokens, proj_weight),
        [
            pl.BlockSpec((tok_rows, row_block), lambda q, o: (0, o[q])),
            pl.BlockSpec((row_block, outs), lambda q, o: (o[q], 0)),
        ],
        [jax.ShapeDtypeStruct(shape, BF16)] * 2,
        [pl.BlockSpec(block, lambda q, o: (0, q)), pl.BlockSpec(block, lambda q, o: (0, o[q]))],
    )


def lay_columns(order, x, live, width):
    def body(order_ref, x_ref, live_ref, out_ref):
        out_ref[...] = (x_ref[...].astype(F32) * live_ref[...]).astype(out_ref.dtype)

    rows, cols = x.shape
    return ordered_call(
        body,
        order,
        (cols // width,),
        (x, live),
        [
            pl.BlockSpec((rows, width), lambda q, o: (0, o[q])),
            pl.BlockSpec((rows, 1), lambda q, o: (0, 0)),
        ],
        jax.ShapeDtypeStruct(x.shape, x.dtype),
        pl.BlockSpec((rows, width), lambda q, o: (0, q)),
    )


def plain_call(body, grid, ins, in_specs, out, out_spec, flops, scratch=()):
    size = sum(x.size * x.dtype.itemsize for x in ins) + out.size * out.dtype.itemsize
    return pl.pallas_call(
        body,
        out_shape=out,
        grid=grid,
        in_specs=in_specs,
        out_specs=out_spec,
        scratch_shapes=scratch,
        compiler_params=pltpu.CompilerParams(vmem_limit_bytes=30 * 1024 * 1024),
        cost_estimate=pl.CostEstimate(flops=flops, bytes_accessed=size, transcendentals=0),
    )(*ins)


def cross_rows(scale, stacked, terms):
    (near_high, near_low), (away_high, away_low) = terms
    rows, depth = stacked.shape[0] // 2, stacked.shape[1]
    cols = near_high.shape[1]
    wide = min(cols, 256)
    half = depth // 2

    def body(scale_ref, rows_ref, nh_ref, nl_ref, ah_ref, al_ref, out_ref):
        wide_part = dot(rows_ref[:, :half], nh_ref[...], 1, 0)
        wide_part += dot(rows_ref[:, half:], ah_ref[...], 1, 0)
        total = wide_part[:rows] + wide_part[rows:]
        total += dot(rows_ref[:rows, :half], nl_ref[...], 1, 0)
        total += dot(rows_ref[:rows, half:], al_ref[...], 1, 0)
        out_ref[...] = total * scale_ref[0, 0]

    panel = pl.BlockSpec((half, wide), lambda j: (0, j))
    return plain_call(
        body,
        (cols // wide,),
        (scale, stacked, near_high, near_low, away_high, away_low),
        [
            pl.BlockSpec(memory_space=pltpu.SMEM),
            pl.BlockSpec((2 * rows, depth), lambda j: (0, 0)),
        ]
        + [panel] * 4,
        jax.ShapeDtypeStruct((rows, cols), F32),
        pl.BlockSpec((rows, wide), lambda j: (0, j)),
        6 * rows * depth * cols,
    )


def add_product(base, factor, levels, chunk, rows, terms):
    (near_high, near_low), (away_high, away_low) = terms
    depth, cols = near_high.shape
    height = base.shape[0]
    loops = rows[0].shape[0]
    wide = min(cols, 256)
    places = lax.axis_size("dp") // 2
    part = depth // loops

    def body(factor_ref, level_ref, base_ref, rh_ref, rl_ref, nh_ref, nl_ref, ah_ref, al_ref, out_ref, kept):
        @pl.when(pl.program_id(0) == 0)
        def _():
            for term, ref in enumerate((rh_ref, rl_ref)):
                for r in range(loops):
                    for h in range(2):
                        kept[term, h, :, r * part : (r + 1) * part] = ref[
                            level_ref[r], :, h * part : (h + 1) * part
                        ]

        def by_level(ref):
            x = ref[...].reshape(places, loops, part // places, wide)
            return jnp.concatenate([x[q, r] for r in range(loops) for q in range(places)], axis=0)

        total = 0.0
        for h, (high_ref, low_ref) in enumerate(((nh_ref, nl_ref), (ah_ref, al_ref))):
            high, low = by_level(high_ref), by_level(low_ref)
            total += dot(kept[0, h], high, 1, 0)
            total += dot(kept[1, h], high, 1, 0)
            total += dot(kept[0, h], low, 1, 0)
        out_ref[...] = base_ref[...] + total * factor_ref[0, 0]

    flat = pl.BlockSpec((height, wide), lambda j: (0, j))
    panel = pl.BlockSpec((depth, wide), lambda j: (0, j))
    strip = pl.BlockSpec((loops, height, 2 * part), lambda j: (0, 0, chunk))
    scalars = pl.BlockSpec(memory_space=pltpu.SMEM)
    return plain_call(
        body,
        (cols // wide,),
        (factor, levels, base, *rows, near_high, near_low, away_high, away_low),
        [scalars, scalars, flat, strip, strip] + [panel] * 4,
        jax.ShapeDtypeStruct(base.shape, F32),
        flat,
        12 * height * depth * cols,
        [pltpu.VMEM((2, 2, height, depth), BF16)],
    )


def on_device(tokens, cotangent, proj_weight, rotation, doc_lengths):
    tok_rows, feat_width = tokens.shape
    slot_count = doc_lengths.shape[0]
    slot_len = tok_rows // slot_count
    n, loops = lax.axis_size("dp"), lax.axis_size("loop")
    half = n // 2
    me, level = lax.axis_index("dp"), lax.axis_index("loop")
    place = (me & 1) * half + (me >> 1)
    masks = relative_masks()
    order = jnp.bitwise_xor(me, jnp.array(masks, jnp.int32))
    places = jnp.bitwise_xor(place, jnp.arange(n, dtype=jnp.int32))
    row_block, panel = rotation.shape
    out_block = proj_weight.shape[1]
    all_tokens, all_outs = tok_rows * n, out_block * n
    chunks = max(1, panel // (n * 64))
    wide = panel // chunks
    sub = wide // n

    rot_top = jnp.maximum(jnp.max(jnp.abs(rotation)), 1e-30)
    rot_power = jnp.floor(14.5 - jnp.log2(rot_top))
    rot_scale, rot_unit = jnp.exp2(rot_power), jnp.exp2(-rot_power)
    rot_round = lax.reduce_precision(rotation, 8, 7)
    code = half_code(rotation, rot_scale)
    inner = half_code(rot_round + 0.75 * (rotation - rot_round), rot_scale)
    read = code * rot_unit
    kept = (lax.reduce_precision(read * (1 + 1e-6), 8, 7) == rot_round) & (
        lax.reduce_precision(read * (1 - 1e-6), 8, 7) == rot_round
    )
    rot_code = jnp.where(kept, code, inner).astype(F16)
    rot_units = jnp.full((128,), rot_unit)
    bit = 1
    while bit < half:
        rot_units = jnp.concatenate([rot_units, swap(rot_units, 2 * bit)], axis=0)
        bit *= 2
    rot_code, rot_units = tie(rot_code, rot_units)
    rot_units = jnp.concatenate([rot_units, swap(rot_units, 1)], axis=0)
    rot_units = rot_units.reshape(2, half, 1, 128)[:, :, :, :1]
    tokens, cotangent, proj_weight, rot_code = tie(tokens, cotangent, proj_weight, rot_code)
    rot_came = first_step(rot_code)

    def decode(part, units):
        part = part.reshape(half, row_block, panel).astype(F32) * units
        return split(part.reshape(half * row_block, panel))

    positions = jnp.arange(tok_rows, dtype=jnp.int32)
    slot_match = (positions // slot_len)[:, None] == jnp.arange(slot_count, dtype=jnp.int32)[
        None, :
    ]
    row_lengths = jnp.sum(jnp.where(slot_match, doc_lengths[None, :], 0), axis=1)
    live_rows = positions % slot_len < row_lengths
    masked = lay_columns(order, cotangent, live_rows.astype(F32)[:, None], out_block)
    both, both_plain = lay_both(order, tokens, proj_weight, row_block)
    cuts = masked.reshape(tok_rows, n, out_block).transpose(1, 0, 2)
    cols = jnp.arange(panel, dtype=jnp.int32)
    source = cols - cols % wide + (((cols % wide) // sub) ^ place) * sub + cols % sub
    shuffle = (cols[:, None] == source[None, :]).astype(BF16)
    rows_terms = [
        dot(x, shuffle, 1, 0).astype(BF16) for x in split(tie(rotation, tokens)[0])
    ]
    rows_sent = rows_terms
    rot_came, cuts, rows_terms, rot_units = tie(rot_came, cuts, rows_terms, rot_units)
    rows_terms = [lax.all_gather(x, "loop", axis=0) for x in rows_sent]
    rot_far = far_step(rot_code, rot_came)
    rot_far, both, both_plain = tie(rot_far, both, both_plain)
    rot_near = join(rot_code, rot_came, rot_far)
    rot_away = swap(rot_near, 1)
    cuts_way = exchange_steps(cuts)
    cuts = next(cuts_way)
    rot_terms = [decode(rot_near, rot_units[0])]
    near_part = dot(both[:, : feat_width // 2], rot_terms[0][0], 1, 0)

    half_feat, half_out = feat_width // 2, all_outs // 2
    rot_away, near_part, cuts = tie(rot_away, near_part, cuts)
    rot_terms.append(decode(rot_away, rot_units[1]))
    cuts = cuts_way.send(cuts)
    rotated = near_part + dot(both[:, half_feat:], rot_terms[1][0], 1, 0)
    acts_raw, mixed_raw = rotated[:tok_rows].astype(BF16), rotated[tok_rows:].astype(BF16)
    power = after(jnp.sum(rotated * rotated, axis=1), acts_raw, mixed_raw)
    acts_came = first_step(acts_raw)
    acts_came, mixed_raw = tie(acts_came, mixed_raw)
    mixed_came = first_step(mixed_raw)
    power = sum_loop(power)
    tokens, proj_weight, rotation = after((tokens, proj_weight, rotation), acts_raw)
    limit = clip_ratio * jnp.sqrt(power / feat_width + eps_power)
    tok_top = jnp.max(jnp.abs(tokens), axis=1).astype(F32)
    weight_top = jnp.max(jnp.abs(proj_weight), axis=0).astype(F32)
    sizes = [
        jnp.sum(limit[tok_rows:] ** 2),
        jnp.sum(limit[:tok_rows] ** 2),
        jnp.sum(tok_top**2),
        jnp.sum(weight_top**2),
        jnp.max(jnp.sum(rotation**2, axis=0)),
    ]
    sizes = jnp.concatenate([jnp.stack(sizes), jnp.zeros((128 - len(sizes),), F32)])
    acts_came, rows_high = tie(acts_came, rows_terms[0])
    rows_terms = [rows_high, rows_terms[1]]
    acts_far = far_step(acts_raw, acts_came)
    told = jnp.concatenate([limit, sizes])
    acts_far, told, cuts = tie(acts_far, told, cuts)
    acts_near = join(acts_raw, acts_came, acts_far)
    acts_away = swap(acts_near, 1)
    told = gather_small(told)
    cot_owned = cuts.reshape(2, half * tok_rows, out_block)
    mixed_near = second_step(mixed_raw, mixed_came)
    mixed_near, told = tie(mixed_near, told)
    told = told.reshape(2, half, -1)
    mixed_away = swap(mixed_near, 1)
    limits = told[:, :, : limit.shape[0]].astype(BF16)
    norms = jnp.sqrt(n * jnp.max(told[:, :, limit.shape[0] :], axis=(0, 1)))
    bound = cot_limit * all_outs**0.5 * (norms[0] * norms[2] + norms[1] * norms[3])
    grad_scale = code_top / jnp.clip(1.02 * bound, 1e-30, 3e38)
    cross_scale = 0.9 / (feat_width**0.5 * jnp.maximum(norms[4], 1e-15))

    shuffle = shuffle[:wide, :wide]
    to_code = grad_scale / jnp.sqrt(F32(all_tokens))

    acts_limit = limits[:, :, :tok_rows].reshape(2, half * tok_rows, 1)
    mixed_limit = limits[:, :, tok_rows:].reshape(2, half * out_block, 1)

    def clip(x, top):
        return jnp.clip(x, -top, top)

    acts_q = [clip(x, top) for x, top in zip((acts_near, acts_away), acts_limit)]
    grad_mixed = sum(dot(x, y, 0, 0) for x, y in zip(cot_owned, acts_q)).astype(BF16)
    mixed_near, mixed_away, grad_mixed, rows_low = tie(
        mixed_near, mixed_away, grad_mixed, rows_terms[1]
    )
    rows_terms = [rows_terms[0], rows_low]
    mixed_q = [clip(x, top) for x, top in zip((mixed_near, mixed_away), mixed_limit)]
    grad_acts = sum(
        dot(masked[:, h * half_out : (h + 1) * half_out], mixed_q[h], 1, 0) for h in range(2)
    ).astype(BF16)
    pairs = jnp.concatenate([grad_acts, grad_mixed], axis=0)

    totals, strips = [], []
    for c in range(chunks):
        pair = pairs[:, c * wide : (c + 1) * wide]
        pair = jnp.dot(pair, shuffle, preferred_element_type=F32).astype(BF16)
        away = (dot(pair[:, wide // 2 :], both_plain, 0, 0) * to_code).astype(F16)
        near = dot(pair[:, : wide // 2], both_plain, 0, 0) * to_code
        totals.append(near + swap(away, 1).astype(F32))
    for c in range(chunks):
        came = scatter_first(totals[c]) if n == 8 else ()
        if c + 1 < chunks:
            totals[c + 1], came = tie(totals[c + 1], came)
        strip = scatter_last(totals[c], came)
        strip = lay_columns(order, strip, jnp.ones((sub, 1), F32), row_block).astype(F16)
        strips.append(strip)

    strip = jnp.concatenate(strips, axis=0)
    blocks = strip.reshape(chunks * sub, n, row_block).transpose(1, 0, 2)
    blocks_way = exchange_steps(blocks)
    blocks = blocks_way.send(next(blocks_way))
    blocks = jnp.concatenate(
        [lax.dynamic_slice_in_dim(blocks, place ^ q, 1, 0) for q in range(n)], axis=0
    )
    gradient = blocks.reshape(n, chunks, sub, row_block).transpose(1, 0, 2, 3)
    unit = 1.0 / grad_scale
    gradient = lax.optimization_barrier(gradient.reshape(panel, row_block).astype(F32) * unit)
    result = gradient.T
    factor = -(unit / cross_scale).reshape(1, 1)

    levels = (level + jnp.arange(loops, dtype=jnp.int32)) % loops

    cross_pairs = []
    for c in range(chunks):
        later = strips[c + 1 : c + 2]
        rows = jnp.concatenate(gather_loop(strips[c], later or None), axis=0)
        strips[c + 1 : c + 2] = later
        if c:
            rows, cross_near = tie(rows, cross_near)
            cross_pairs.append((cross_near, swap(cross_near, 1)))
        stacked = jnp.concatenate(split(rows.astype(F32)), axis=0)
        cross = cross_rows(cross_scale.reshape(1, 1), stacked, rot_terms).astype(F16)
        came = first_step(cross)
        if c + 1 < chunks:
            cross_near = second_step(cross, came)
    for c, pair in enumerate(cross_pairs):
        result = add_product(result, factor, levels, c, rows_terms, [split(x.astype(F32)) for x in pair])
    came, result = tie(came, result)
    far = far_step(cross, came)
    cross_near = join(cross, came, far)
    pair = (cross_near, swap(cross_near, 1))
    terms = [split(x.astype(F32)) for x in pair]
    result = add_product(result, factor, levels, chunks - 1, rows_terms, terms)
    return result


def solution(mesh):
    in_specs = (P("dp", None), P("dp", None), P(None, "dp"), P("dp", "loop"), P("dp"))
    out_specs = P("dp", "loop")
    return jax.shard_map(
        on_device, mesh=mesh, in_specs=in_specs, out_specs=out_specs, check_vma=False
    )
```
